256 devices in a mesh: dp: 16 (over z_hi, x), expert: 16 (over z_lo, y, core).
Axes of the slice: x: 4, y: 4, z: 8 (z_hi: 4, z_lo: 2; z = z_hi * 2 + z_lo), core: 2. Of those that a mesh axis runs over, the one named last changes fastest.
Arguments:
- tokens: bfloat16 [512, 256, 1280], P(('dp', 'expert')), may hold values from -6 to 6
- logits: float32 [512, 256, 32], P(('dp', 'expert')), may hold values from -20 to 320
- out_grad: bfloat16 [512, 256, 1280], P(('dp', 'expert')), may hold values from -6 to 6
- w_in: bfloat16 [32, 5120, 1280], P('expert', 'dp'), may hold values from -0.15625 to 0.15625
- w_out: bfloat16 [32, 5120, 1280], P('expert', 'dp'), may hold values from -0.078125 to 0.078125
Outputs:
- token_grad: bfloat16 [512, 256, 1280], P(('dp', 'expert'))
- logit_grad: float32 [512, 256, 32], P(('dp', 'expert'))
- w_in_grad: bfloat16 [32, 5120, 1280], P('expert', 'dp')
- w_out_grad: bfloat16 [32, 5120, 1280], P('expert', 'dp')
The draws below stay inside these ranges and needn't reach their ends.
All inputs are finite; a program needn't handle non-finite values.
Results may differ from the reference program's by a relative error of at most 0.008.
Values may be sent and summed in bfloat16 or wider, within the bound.
A program may use at most 128 MiB of HBM per device.

```python
import jax
import jax.numpy as jnp
from jax import lax

D = 1280
FF = 5120
TOKENS_IMG = 256
EXPERTS = 32
IMAGES = 512


def draw_logits(key, part):
    key = jax.random.fold_in(key, 7)
    first = jax.random.fold_in(key, 0)
    shape = (IMAGES, TOKENS_IMG, EXPERTS)
    return jnp.clip(3.0 * jax.random.normal(first, shape, jnp.float32), -20.0, 20.0)


def block_levels(rng, extent, shards, least, largest):
    def one(axis_at, blocks):
        steps = jax.random.uniform(jax.random.fold_in(jax.random.fold_in(rng, 6), axis_at), (blocks,), jnp.float32, least / len(shards), largest / len(shards))
        return jnp.repeat(jnp.exp(steps), extent[axis_at] // blocks).reshape((-1,) + (1,) * (len(extent) - axis_at - 1))

    gain = one(*shards[0])
    for cut in shards[1:]:
        gain = gain * one(*cut)
    return gain


def gaussian(stream_key, extent, deviation, limit, shards=(), held_as=jnp.bfloat16):
    drawn = jax.random.normal(stream_key, extent, jnp.float32) * deviation
    if len(shards) > 0:
        drawn = block_levels(stream_key, extent, shards, -0.22, 0.18) * drawn
    return jnp.clip(drawn, min=-limit, max=limit).astype(held_as)


def setup_inputs(seed: int = 0) -> dict:
    key_list = jax.random.split(jax.random.key(seed), 6)
    tokens = gaussian(key_list[0], (IMAGES, TOKENS_IMG, D), 1.0, 6.0, ((0, 256),))
    logits = draw_logits(jax.random.fold_in(key_list[5], 71), 0)
    out_grad = gaussian(key_list[2], (IMAGES, TOKENS_IMG, D), 1.0, 6.0, ((0, 256),))
    w_in = gaussian(key_list[3], (EXPERTS, FF, D), D ** -0.5, 0.15625, ((0, 16), (1, 16)))
    w_out = gaussian(key_list[4], (EXPERTS, FF, D), FF ** -0.5, 0.078125, ((0, 16), (1, 16)))
    return dict(tokens=tokens, logits=logits, out_grad=out_grad, w_in=w_in, w_out=w_out)


def soft_weights(values, over_dim):
    highest = jnp.max(values, axis=over_dim, keepdims=True)
    raised = jnp.exp(values - highest)
    return raised / jnp.sum(raised, axis=over_dim, keepdims=True)


def normal_cdf(values):
    return 0.5 * (1.0 + lax.erf(values * 0.7071067811865476))


def gelu_slope(values):
    return normal_cdf(values) + values * jnp.exp(-0.5 * values * values) * 0.3989422804014327


def make_slots(inputs):
    image_tokens, image_logits, image_grad = inputs
    dispatch_b = soft_weights(image_logits, 0).astype(jnp.bfloat16)
    combine_b = soft_weights(image_logits, 1).astype(jnp.bfloat16)
    slot_in = jnp.dot(dispatch_b.T, image_tokens, preferred_element_type=jnp.float32).astype(jnp.bfloat16)
    slot_grad = jnp.dot(combine_b.T, image_grad, preferred_element_type=jnp.float32).astype(jnp.bfloat16)
    return slot_in, slot_grad


def one_expert(inputs):
    slot_rows, grad_rows, weight_in, weight_out = inputs
    pre = jnp.dot(slot_rows, weight_in.T, preferred_element_type=jnp.float32)
    hidden = (pre * normal_cdf(pre)).astype(jnp.bfloat16)
    slot_out = jnp.dot(hidden, weight_out, preferred_element_type=jnp.float32).astype(jnp.bfloat16)
    hidden_grad = jnp.dot(grad_rows, weight_out.T, preferred_element_type=jnp.float32)
    pre_grad = (hidden_grad * gelu_slope(pre)).astype(jnp.bfloat16)
    w_out_grad = jnp.dot(hidden.T, grad_rows, preferred_element_type=jnp.float32).astype(jnp.bfloat16)
    w_in_grad = jnp.dot(pre_grad.T, slot_rows, preferred_element_type=jnp.float32).astype(jnp.bfloat16)
    slot_in_grad = jnp.dot(pre_grad, weight_in, preferred_element_type=jnp.float32).astype(jnp.bfloat16)
    return slot_out, slot_in_grad, w_in_grad, w_out_grad


def finish_image(inputs):
    image_tokens, image_logits, image_grad, slot_out, slot_in_grad = inputs
    dispatch = soft_weights(image_logits, 0)
    combine = soft_weights(image_logits, 1)
    combine_grad = jnp.dot(image_grad, slot_out.T, preferred_element_type=jnp.float32)
    dispatch_grad = jnp.dot(image_tokens, slot_in_grad.T, preferred_element_type=jnp.float32)
    token_grad = jnp.dot(dispatch.astype(jnp.bfloat16), slot_in_grad, preferred_element_type=jnp.float32).astype(jnp.bfloat16)
    from_combine = combine * (combine_grad - jnp.sum(combine * combine_grad, axis=1, keepdims=True))
    from_dispatch = dispatch * (dispatch_grad - jnp.sum(dispatch * dispatch_grad, axis=0, keepdims=True))
    return token_grad, from_combine + from_dispatch


def reference(tokens, logits, out_grad, w_in, w_out):
    slot_in, slot_grad = lax.map(make_slots, (tokens, logits, out_grad))
    slot_out, slot_in_grad, w_in_grad, w_out_grad = lax.map(
        one_expert, (jnp.transpose(slot_in, (1, 0, 2)), jnp.transpose(slot_grad, (1, 0, 2)), w_in, w_out))
    slot_out = jnp.transpose(slot_out, (1, 0, 2))
    slot_in_grad = jnp.transpose(slot_in_grad, (1, 0, 2))
    token_grad, logit_grad = lax.map(finish_image, (tokens, logits, out_grad, slot_out, slot_in_grad))
    return (token_grad, logit_grad, w_in_grad, w_out_grad)
```

```python
import functools

import jax
import jax.numpy as jnp
from jax import lax
from jax.experimental import pallas as pl
from jax.experimental.pallas import tpu as pltpu
from jax.sharding import PartitionSpec as P

NX = 4
NZ = 4


def soft_weights(values, over_dim):
    highest = jnp.max(values, axis=over_dim, keepdims=True)
    raised = jnp.exp(values - highest)
    return raised / jnp.sum(raised, axis=over_dim, keepdims=True)


def normal_cdf(values):
    return 0.5 * (1.0 + lax.erf(values * 0.7071067811865476))


def shift(at, by, size):
    return lax.rem(at + (by + size), size)


def expert_kernel(
    own_ref, w_in_ref, w_out_ref,
    out_ref, w_in_grad_ref, w_out_grad_ref,
    rows, part, x_half, x_full, z_half, z_full,
    w_in, w_out, slope, hidden, pre_grad, w_in_grad, w_out_grad,
    local_sem, send_sem, recv_sem,
):
    members, count, depth = rows.shape[3:]
    me = lax.axis_index("dp")
    z, x = me // NX, lax.rem(me, NX)
    x_to = (shift(x, 1, NX), shift(x, -1, NX))
    x_from = (shift(x, -1, NX), shift(x, 1, NX))
    z_to = (shift(z, 1, NZ), shift(z, -1, NZ))
    z_from = (shift(z, -1, NZ), shift(z, 1, NZ))
    x_across, z_across = shift(x, 2, NX), shift(z, 2, NZ)
    x_dev = tuple(z * NX + to for to in x_to)
    z_dev = tuple(to * NX + x for to in z_to)
    chunk = (z, z_from[0], z_from[1], z_across)

    barrier = pltpu.get_barrier_semaphore()
    for to in x_dev + z_dev:
        pl.semaphore_signal(barrier, inc=1, device_id={"dp": to}, device_id_type=pl.DeviceIdType.MESH)

    loads = [
        pltpu.make_async_copy(own_ref.at[kind], rows.at[kind, z, x], local_sem.at[kind])
        for kind in range(2)
    ]
    loads.append(pltpu.make_async_copy(w_in_ref, w_in, local_sem.at[2]))
    loads.append(pltpu.make_async_copy(w_out_ref, w_out, local_sem.at[3]))
    for load in loads:
        load.start()
    pl.semaphore_wait(barrier, 4)

    sent = []
    used = {}

    def send(key, source, target, device):
        at = len(sent)
        copy = pltpu.make_async_remote_copy(
            src_ref=source, dst_ref=target,
            send_sem=send_sem.at[at], recv_sem=recv_sem.at[at],
            device_id={"dp": device}, device_id_type=pl.DeviceIdType.MESH,
        )
        copy.start()
        sent.append(copy)
        used[key] = copy

    def arrived(key):
        used.pop(key).wait_recv()

    def gather_z1(kind):
        block = rows.at[kind, z, x]
        for way in range(2):
            send(("gz1", kind, way), block, block, z_dev[way])

    def gather_z2(kind, way):
        arrived(("gz1", kind, way))
        half = rows.at[kind, z_from[way], x, way]
        send(("gz2", kind, way), half, half, z_dev[way])

    def gather_z3(kind):
        for way in range(2):
            arrived(("gz2", kind, way))

    def gather_x1(kind, c):
        block = rows.at[kind, chunk[c], x]
        for way in range(2):
            send(("gx1", kind, c, way), block, block, x_dev[way])

    def gather_x2(kind, c):
        for way in range(2):
            arrived(("gx1", kind, c, way))
            half = rows.at[kind, chunk[c], x_from[way], way]
            send(("gx2", kind, c, way), half, half, x_dev[way])

    def gather_x3(kind, c):
        for way in range(2):
            arrived(("gx2", kind, c, way))

    def plus(*refs):
        total = refs[0][...].astype(jnp.float32)
        for ref in refs[1:]:
            total = total + ref[...].astype(jnp.float32)
        return total.astype(jnp.bfloat16)

    def reduce_x1(kind, c):
        for way in range(2):
            send(("rx1", kind, c, way), part.at[kind, chunk[c], x_across, way],
                 x_half.at[kind, c, way], x_dev[way])

    def reduce_x2(kind, c):
        for way in range(2):
            arrived(("rx1", kind, c, way))
            mine = part.at[kind, chunk[c], x_to[way]]
            mine[way] = plus(mine.at[way], x_half.at[kind, c, way])
            send(("rx2", kind, c, way), mine, x_full.at[kind, c, way], x_dev[way])

    def reduce_x3(kind, c):
        for way in range(2):
            arrived(("rx2", kind, c, way))
        mine = part.at[kind, chunk[c], x]
        mine[...] = plus(mine, x_full.at[kind, c, 0], x_full.at[kind, c, 1])

    def reduce_z1(kind):
        for way in range(2):
            send(("rz1", kind, way), part.at[kind, z_across, x, way],
                 z_half.at[kind, way], z_dev[way])

    def reduce_z2(kind, way):
        arrived(("rz1", kind, way))
        mine = part.at[kind, z_to[way], x]
        mine[way] = plus(mine.at[way], z_half.at[kind, way])
        send(("rz2", kind, way), mine, z_full.at[kind, way], z_dev[way])

    def reduce_z3(kind):
        for way in range(2):
            arrived(("rz2", kind, way))
        out_ref[kind] = plus(part.at[kind, z, x], z_full.at[kind, 0], z_full.at[kind, 1])

    def chunk_rows(kind, c, e):
        return rows[kind, chunk[c], :, e].reshape(NX * count, depth)

    def place(c):
        return pl.ds(pl.multiple_of(chunk[c] * (NX * count), NX * count), NX * count)

    def forward(c):
        for e in range(members):
            pre = lax.dot_general(chunk_rows(0, c, e), w_in[e], (((1,), (1,)), ((), ())),
                                  preferred_element_type=jnp.float32)
            cdf = normal_cdf(pre)
            act = (pre * cdf).astype(jnp.bfloat16)
            slope[e, place(c)] = cdf + pre * jnp.exp(-0.5 * pre * pre) * 0.3989422804014327
            hidden[e, place(c)] = act
            out = jnp.dot(act, w_out[e], preferred_element_type=jnp.float32)
            part[0, chunk[c], :, e] = out.astype(jnp.bfloat16).reshape(NX, count, depth)

    def backward(c):
        for e in range(members):
            grad = lax.dot_general(chunk_rows(1, c, e), w_out[e], (((1,), (1,)), ((), ())),
                                   preferred_element_type=jnp.float32)
            grad = (grad * slope[e, place(c)]).astype(jnp.bfloat16)
            pre_grad[e, place(c)] = grad
            out = jnp.dot(grad, w_in[e], preferred_element_type=jnp.float32)
            part[1, chunk[c], :, e] = out.astype(jnp.bfloat16).reshape(NX, count, depth)

    def weight_grad(left, kind, e, target):
        right = rows[kind, :, :, e].reshape(NZ * NX * count, depth)
        target[e] = lax.dot_general(left[e], right, (((0,), (0,)), ((), ())),
                                    preferred_element_type=jnp.float32).astype(jnp.bfloat16)

    loads[0].wait()
    gather_z1(0)
    gather_x1(0, 0)
    loads[1].wait()
    gather_z2(0, 0)
    gather_x1(0, 1)
    gather_z2(0, 1)
    gather_x1(0, 2)
    gather_x2(0, 0)
    gather_z1(1)
    gather_z3(0)
    gather_x1(0, 3)
    gather_x2(0, 1)
    gather_x1(1, 0)
    gather_x2(0, 2)
    gather_z2(1, 0)
    gather_x1(1, 1)
    gather_z2(1, 1)
    gather_x1(1, 2)
    loads[2].wait()
    loads[3].wait()
    gather_x3(0, 0)
    forward(0)
    gather_x2(0, 3)
    gather_z3(1)
    gather_x1(1, 3)
    gather_x3(0, 1)
    forward(1)
    gather_x2(1, 0)
    gather_x3(0, 2)
    forward(2)
    gather_x2(1, 1)
    gather_x3(0, 3)
    forward(3)
    gather_x2(1, 2)
    reduce_x1(0, 3)
    gather_x2(1, 3)
    reduce_x1(0, 1)
    reduce_x1(0, 2)
    reduce_x1(0, 0)
    gather_x3(1, 0)
    backward(0)
    reduce_x2(0, 3)
    gather_x3(1, 1)
    backward(1)
    reduce_x2(0, 1)
    gather_x3(1, 2)
    backward(2)
    reduce_x2(0, 2)
    reduce_x3(0, 3)
    reduce_z1(0)
    gather_x3(1, 3)
    backward(3)
    reduce_x1(1, 3)
    reduce_x2(0, 0)
    reduce_x3(0, 1)
    reduce_z2(0, 1)
    reduce_x1(1, 1)
    reduce_x3(0, 2)
    reduce_z2(0, 0)
    reduce_x1(1, 2)
    reduce_x1(1, 0)
    weight_grad(hidden, 1, 0, w_out_grad)
    reduce_x2(1, 3)
    reduce_x3(0, 0)
    weight_grad(hidden, 1, 1, w_out_grad)
    stores = [pltpu.make_async_copy(w_out_grad, w_out_grad_ref, local_sem.at[4])]
    stores[0].start()
    reduce_x2(1, 1)
    reduce_x3(1, 3)
    reduce_z1(1)
    reduce_x2(1, 2)
    reduce_z3(0)
    weight_grad(pre_grad, 0, 0, w_in_grad)
    reduce_x2(1, 0)
    reduce_x3(1, 1)
    reduce_z2(1, 1)
    reduce_x3(1, 2)
    reduce_z2(1, 0)
    weight_grad(pre_grad, 0, 1, w_in_grad)
    stores.append(pltpu.make_async_copy(w_in_grad, w_in_grad_ref, local_sem.at[5]))
    stores[1].start()
    reduce_x3(1, 0)
    reduce_z3(1)
    for copy in sent:
        copy.wait_send()
    for store in stores:
        store.wait()


COPIES = 2 * 2 * (4 + 4 * 4)


def experts(own, w_in, w_out):
    members, width, depth = w_in.shape
    count = own.shape[2]
    block = (members, count, depth)
    half = (count, depth)
    kept = (members, NZ * NX * count, width)
    bf16 = jnp.bfloat16
    return pl.pallas_call(
        expert_kernel,
        out_shape=(
            jax.ShapeDtypeStruct(own.shape, bf16),
            jax.ShapeDtypeStruct(w_in.shape, bf16),
            jax.ShapeDtypeStruct(w_out.shape, bf16),
        ),
        in_specs=[pl.BlockSpec(memory_space=pl.ANY)] * 3,
        out_specs=(
            pl.BlockSpec(memory_space=pltpu.VMEM),
            pl.BlockSpec(memory_space=pl.ANY),
            pl.BlockSpec(memory_space=pl.ANY),
        ),
        scratch_shapes=[
            pltpu.VMEM((2, NZ, NX) + block, bf16),
            pltpu.VMEM((2, NZ, NX) + block, bf16),
            pltpu.VMEM((2, NZ, 2) + half, bf16),
            pltpu.VMEM((2, NZ, 2) + block, bf16),
            pltpu.VMEM((2, 2) + half, bf16),
            pltpu.VMEM((2, 2) + block, bf16),
            pltpu.VMEM(w_in.shape, bf16),
            pltpu.VMEM(w_out.shape, bf16),
            pltpu.VMEM(kept, jnp.float32),
            pltpu.VMEM(kept, bf16),
            pltpu.VMEM(kept, bf16),
            pltpu.VMEM(w_in.shape, bf16),
            pltpu.VMEM(w_out.shape, bf16),
            pltpu.SemaphoreType.DMA((6,)),
            pltpu.SemaphoreType.DMA((COPIES,)),
            pltpu.SemaphoreType.DMA((COPIES,)),
        ],
        compiler_params=pltpu.CompilerParams(
            collective_id=0, has_side_effects=True, vmem_limit_bytes=50 * 2**20
        ),
    )(own, w_in, w_out)


def shards(tokens, logits, out_grad, w_in, w_out):
    dispatch = soft_weights(logits, 1)
    combine = soft_weights(logits, 2)
    dispatch_b = dispatch.astype(jnp.bfloat16)
    combine_b = combine.astype(jnp.bfloat16)
    slot_in = jnp.einsum(
        "ims,imd->isd", dispatch_b, tokens, preferred_element_type=jnp.float32
    ).astype(jnp.bfloat16)
    slot_grad = jnp.einsum(
        "ims,imd->isd", combine_b, out_grad, preferred_element_type=jnp.float32
    ).astype(jnp.bfloat16)
    images, slots, depth = slot_in.shape
    group = lax.axis_size("expert")
    members = slots // group
    packed = jnp.stack((slot_in, slot_grad)).reshape(2, images, group, members, depth)
    packed = jnp.transpose(packed, (2, 0, 3, 1, 4))
    owned = lax.all_to_all(packed, "expert", split_axis=0, concat_axis=0, tiled=True)
    owned = jnp.transpose(owned, (1, 2, 0, 3, 4)).reshape(2, members, group * images, depth)
    summed, w_in_grad, w_out_grad = experts(owned, w_in, w_out)
    summed = jnp.transpose(summed.reshape(2, members, group, images, depth), (2, 0, 1, 3, 4))
    back = lax.all_to_all(summed, "expert", split_axis=0, concat_axis=0, tiled=True)
    back = jnp.transpose(back, (1, 3, 0, 2, 4)).reshape(2, images, slots, depth)
    slot_out, slot_in_grad = back[0], back[1]
    combine_grad = jnp.einsum(
        "imd,isd->ims", out_grad, slot_out, preferred_element_type=jnp.float32
    )
    dispatch_grad = jnp.einsum(
        "imd,isd->ims", tokens, slot_in_grad, preferred_element_type=jnp.float32
    )
    token_grad = jnp.einsum(
        "ims,isd->imd", dispatch_b, slot_in_grad, preferred_element_type=jnp.float32
    ).astype(jnp.bfloat16)
    from_combine = combine * (combine_grad - jnp.sum(combine * combine_grad, axis=2, keepdims=True))
    from_dispatch = dispatch * (
        dispatch_grad - jnp.sum(dispatch * dispatch_grad, axis=1, keepdims=True)
    )
    return (token_grad, from_combine + from_dispatch, w_in_grad, w_out_grad)


def solution(mesh):
    placed = (
        P(("dp", "expert"), None, None),
        P(("dp", "expert"), None, None),
        P(("dp", "expert"), None, None),
        P("expert", "dp", None),
        P("expert", "dp", None),
    )
    return jax.shard_map(
        shards,
        mesh=mesh,
        in_specs=placed,
        out_specs=(
            P(("dp", "expert"), None, None),
            P(("dp", "expert"), None, None),
            P("expert", "dp", None),
            P("expert", "dp", None),
        ),
        check_vma=False,
    )
```

```python
import jax
import jax.numpy as jnp
from jax import lax
from jax.experimental import pallas as pl
from jax.experimental.pallas import tpu as pltpu
from jax.sharding import PartitionSpec as P

RING = 4
TILE = 128
SPLIT = 1024
MESH = pl.DeviceIdType.MESH
BF16 = jnp.bfloat16
F32 = jnp.float32


def normal_cdf(values):
    return 0.5 * (1.0 + lax.erf(values * 0.7071067811865476))


def soft_weights(values, over_dim):
    highest = jnp.max(values, axis=over_dim, keepdims=True)
    raised = jnp.exp(values - highest)
    return raised / jnp.sum(raised, axis=over_dim, keepdims=True)


def shift(at, by, size):
    return lax.rem(at + (by + size), size)


def iota(shape, dim):
    return lax.broadcasted_iota(jnp.int32, shape, dim)


class Plan:
    LATENCY = 2.0
    RATE = {"x": 0.05, "z": 0.025, "y": 0.05}

    def __init__(self):
        self.tasks = {}
        self.sends = {}

    def add(self, name, rank, cost, needs, run, sends=()):
        self.tasks[name] = (rank, cost, tuple(needs), run)
        self.sends[name] = tuple(sends)

    def order(self):
        left = dict(self.tasks)
        done, arrives, free, now = {}, {}, {}, 0.0
        listed = []
        while left:
            best = None
            for name, (rank, cost, needs, run) in left.items():
                if not all(need in done or need in arrives for need in needs):
                    continue
                ready = max([now] + [arrives[need] for need in needs if need in arrives])
                key = (ready, rank)
                if best is None or key < best[0]:
                    best = (key, name)
            (start, _), name = best
            rank, cost, needs, run = left.pop(name)
            now = start + cost
            done[name] = now
            for message, link, size in self.sends[name]:
                begin = max(now, free.get(link, 0.0))
                free[link] = begin + size / self.RATE[link[0]]
                arrives[message] = free[link] + self.LATENCY
            listed.append((start, name, run))
        self.length = max(now, max(arrives.values()))
        return listed


def kernel(
    tokens_ref, logits_ref, out_grad_ref, w_in_ref, w_out_ref,
    token_grad_ref, logit_grad_ref, w_in_grad_ref, w_out_grad_ref,
    tokens, out_grad, dispatch, combine, outbox, inbox, back_outbox, back_inbox,
    rows, part, half_a, full_a, half_b, full_b, last_half, last_full, total,
    w_in, w_out, slope, hidden, pre_grad, w_in_grad, w_out_grad,
    load_sem, store_sem, swap_send, swap_recv, send_sem, recv_sem,
):
    members, count, depth = rows.shape[3:]
    images, length, slots = dispatch.shape
    group = slots // members
    packed = group * 2 * images * members
    me = lax.axis_index("dp")
    mine = lax.axis_index("expert")
    at = {"z": me // RING, "x": lax.rem(me, RING)}
    to = {axis: (shift(at[axis], 1, RING), shift(at[axis], -1, RING)) for axis in "zx"}
    come = {axis: (to[axis][1], to[axis][0]) for axis in "zx"}
    across = {axis: shift(at[axis], 2, RING) for axis in "zx"}
    device = {
        "z": tuple(z * RING + at["x"] for z in to["z"]),
        "x": tuple(at["z"] * RING + x for x in to["x"]),
    }
    chunk = {axis: (at[axis], come[axis][0], come[axis][1], across[axis]) for axis in "zx"}
    halves = (
        ("z", "x", pl.ds(0, SPLIT)),
        ("x", "z", pl.ds(SPLIT, depth - SPLIT)),
    )
    width = (SPLIT, depth - SPLIT)
    half_buf, full_buf = (half_a, half_b), (full_a, full_b)

    def partner(by):
        return lax.rem(mine + by, group)

    barrier = pltpu.get_barrier_semaphore()
    for axis in "zx":
        for there in device[axis]:
            pl.semaphore_signal(barrier, inc=1, device_id={"dp": there}, device_id_type=MESH)

    def greet(by, carry):
        pl.semaphore_signal(barrier, inc=1, device_id={"expert": partner(by)}, device_id_type=MESH)
        return carry

    lax.fori_loop(1, group, greet, 0)

    loads = [
        pltpu.make_async_copy(source, target, load_sem.at[i])
        for i, (source, target) in enumerate(
            ((tokens_ref, tokens), (out_grad_ref, out_grad), (w_in_ref, w_in), (w_out_ref, w_out))
        )
    ]
    for load in loads:
        load.start()

    def tiled(block):
        pieces = [
            block[:, at_column * TILE:(at_column + 1) * TILE].reshape(group, 1, 8, TILE)
            for at_column in range(depth // 2 // TILE)
        ]
        if len(pieces) % 2:
            pieces.append(jnp.zeros_like(pieces[0]))
        return jnp.concatenate(pieces, axis=1).reshape(group, len(pieces) * 8, TILE).astype(BF16)

    def untiled(block):
        pieces = block.astype(F32).reshape(group, block.shape[1] // 8, 8, TILE)
        return jnp.concatenate(
            [pieces[:, i].reshape(packed, TILE) for i in range(depth // 2 // TILE)], axis=1
        ).astype(BF16)

    def swap_copy(kind, way, by, box, inbound):
        return pltpu.make_async_remote_copy(
            src_ref=box.at[kind, partner(by)], dst_ref=inbound.at[kind, mine],
            send_sem=swap_send.at[way, kind, by], recv_sem=swap_recv.at[way, kind, by],
            device_id={"expert": partner(by)}, device_id_type=MESH,
        )

    def swap_start(kind, way, box, inbound):
        def one(by, carry):
            swap_copy(kind, way, by, box, inbound).start()
            return carry

        lax.fori_loop(1, group, one, 0)
        inbound[kind, mine] = box[kind, mine]

    def swap_arrived(kind, way, box, inbound):
        def one(by, carry):
            swap_copy(kind, way, by, box, inbound).wait_recv()
            return carry

        lax.fori_loop(1, group, one, 0)

    def picker(half, by_member):
        shape = (packed // 2, packed)
        row, column = iota(shape, 0), iota(shape, 1)
        first, source, second = row // (packed // 4), (row % (packed // 4)) // 2, row % 2
        image, member = (second, first) if by_member else (first, second)
        return (column == ((source * 2 + half) * 2 + image) * 2 + member).astype(F32).astype(BF16)

    def unpack(block, by_member):
        block = untiled(block)
        return jnp.concatenate(
            [jnp.dot(picker(half, by_member), block, preferred_element_type=F32) for half in range(2)],
            axis=1,
        ).astype(BF16)

    def pack(block):
        return sum(
            lax.dot_general(picker(half, True), block[:, half * depth // 2:(half + 1) * depth // 2],
                            (((0,), (0,)), ((), ())), preferred_element_type=F32)
            for half in range(2)
        )

    def spread(image):
        slot, column = iota((slots, packed), 0), iota((slots, packed), 1)
        same = (slot == (column // 8) * 2 + column % 2) & ((column // 2) % 2 == image)
        return same.astype(F32).astype(BF16)

    def make_slots(kind):
        source, weights = ((tokens, dispatch), (out_grad, combine))[kind]
        left = []
        for image in range(images):
            soft = soft_weights(logits_ref[image], kind)
            weights[image] = soft
            left.append(
                jnp.dot(soft.astype(BF16), spread(image), preferred_element_type=F32).astype(BF16))
        loads[kind].wait()
        slot = lax.dot_general(
            jnp.concatenate(left, axis=0), source[...].reshape(images * length, depth),
            (((0,), (0,)), ((), ())), preferred_element_type=F32)
        first = (iota((packed, depth // 2), 0) // 4) % 2 == 0
        outbox[kind] = tiled(jnp.where(first, slot[:, :depth // 2], slot[:, depth // 2:]))

    def own_rows(kind):
        swap_arrived(kind, 0, outbox, inbox)
        rows[kind, at["z"], at["x"]] = unpack(inbox[kind], True).reshape(members, count, depth)

    def send_back(kind):
        back_outbox[kind] = tiled(pack(total[kind].reshape(members * count, depth)))
        swap_start(kind, 1, back_outbox, back_inbox)

    def finish(kind):
        swap_arrived(kind, 1, back_outbox, back_inbox)
        slot = unpack(back_inbox[kind], False)
        source, weights = ((out_grad, combine), (tokens, dispatch))[kind]
        for image in range(images):
            back = slot[image * slots:(image + 1) * slots]
            grad = lax.dot_general(source[image], back, (((1,), (1,)), ((), ())),
                                   preferred_element_type=F32)
            soft = weights[image]
            grad = soft * (grad - jnp.sum(soft * grad, axis=1 - kind, keepdims=True))
            if kind == 0:
                logit_grad_ref[image] = grad
            else:
                logit_grad_ref[image] += grad
                token_grad_ref[image] = jnp.dot(
                    soft.astype(BF16), back, preferred_element_type=F32).astype(BF16)

    sent = []
    flying = {}

    def send(key, source, target, there):
        copy = pltpu.make_async_remote_copy(
            src_ref=source, dst_ref=target,
            send_sem=send_sem.at[len(sent)], recv_sem=recv_sem.at[len(sent)],
            device_id={"dp": there}, device_id_type=MESH,
        )
        copy.start()
        sent.append(copy)
        flying[key] = copy

    def arrived(key):
        flying.pop(key).wait_recv()

    def block(ref, kind, p, first, second, member=None):
        z, x = (first, second) if halves[p][0] == "z" else (second, first)
        return ref.at[kind, z, x, slice(None) if member is None else member, :, halves[p][2]]

    plan = Plan()
    size = [members * count * w * 2e-6 for w in width]

    def both(key, axis, megabytes):
        return [(key + (way,), axis + "+-"[way], megabytes) for way in range(2)]

    def gather(kind, p):
        one, two, _ = halves[p]
        own = ("own", kind)
        rank = 10 * kind + p

        def along_one():
            mine_here = block(rows, kind, p, at[one], at[two])
            for way in range(2):
                send(("g1", kind, p, way), mine_here, mine_here, device[one][way])

        plan.add(("g1", kind, p), rank, 0.1, [own], along_one, both(("g1", kind, p), one, size[p]))
        for way in range(2):
            def on_one(way=way):
                arrived(("g1", kind, p, way))
                piece = block(rows, kind, p, come[one][way], at[two], way)
                send(("g2", kind, p, way), piece, piece, device[one][way])

            plan.add(("g2t", kind, p, way), rank, 0.1, [("g1", kind, p, way)], on_one,
                     [(("g2", kind, p, way), one + "+-"[way], size[p] / 2)])

        for c in range(RING):
            needs = ([own], [("g2t", kind, p, 0)], [("g2t", kind, p, 1)],
                     [("g2", kind, p, 0), ("g2", kind, p, 1)])[c]

            def along_two(c=c):
                if c == 3:
                    for way in range(2):
                        arrived(("g2", kind, p, way))
                here = block(rows, kind, p, chunk[one][c], at[two])
                for way in range(2):
                    send(("s1", kind, p, c, way), here, here, device[two][way])

            plan.add(("s1", kind, p, c), rank + 2, 0.1, needs, along_two,
                     both(("s1", kind, p, c), two, size[p]))
            for way in range(2):
                def on_two(c=c, way=way):
                    arrived(("s1", kind, p, c, way))
                    piece = block(rows, kind, p, chunk[one][c], come[two][way], way)
                    send(("s2", kind, p, c, way), piece, piece, device[two][way])

                plan.add(("s2t", kind, p, c, way), rank + 4, 0.1, [("s1", kind, p, c, way)], on_two,
                         [(("s2", kind, p, c, way), two + "+-"[way], size[p] / 2)])

            def gathered(c=c):
                for way in range(2):
                    arrived(("s2", kind, p, c, way))

            plan.add(("g", kind, p, c), rank + 5, 0.05,
                     [("s2t", kind, p, c, 0), ("s2t", kind, p, c, 1),
                      ("s2", kind, p, c, 0), ("s2", kind, p, c, 1)], gathered)

    def plus(*refs):
        value = refs[0][...].astype(F32)
        for ref in refs[1:]:
            value = value + ref[...].astype(F32)
        return value.astype(BF16)

    def reduce(kind, p):
        one, two, features = halves[p]
        half_in, full_in = half_buf[p], full_buf[p]
        rank = 30 + 10 * kind + p
        cost = 0.5 * width[p] / depth
        computed = [("part", kind, c, e) for c in range(RING) for e in range(members)]
        for c in range(RING):
            needs = [("part", kind, c, e) for e in range(members)] if p == 0 else computed
            late = (4, 2, 2, 0)[c]

            def away(c=c):
                for way in range(2):
                    send(("r1", kind, p, c, way),
                         block(part, kind, p, chunk[one][c], across[two], way),
                         half_in.at[kind, c, way], device[two][way])

            plan.add(("r1", kind, p, c), rank + late, 0.1, needs, away,
                     both(("r1", kind, p, c), two, size[p] / 2))
            for way in range(2):
                def add_on(c=c, way=way):
                    arrived(("r1", kind, p, c, way))
                    piece = block(part, kind, p, chunk[one][c], to[two][way], way)
                    piece[...] = plus(piece, half_in.at[kind, c, way])
                    send(("r2", kind, p, c, way), block(part, kind, p, chunk[one][c], to[two][way]),
                         full_in.at[kind, c, way], device[two][way])

                plan.add(("r2t", kind, p, c, way), rank + late, cost / 2, [("r1", kind, p, c, way)],
                         add_on, [(("r2", kind, p, c, way), two + "+-"[way], size[p])])

            def summed(c=c):
                for way in range(2):
                    arrived(("r2", kind, p, c, way))
                here = block(part, kind, p, chunk[one][c], at[two])
                here[...] = plus(here, full_in.at[kind, c, 0], full_in.at[kind, c, 1])

            plan.add(("r", kind, p, c), rank + late, cost,
                     [("r2", kind, p, c, 0), ("r2", kind, p, c, 1)], summed)

        last_h = last_half.at[kind, :, :, features]
        last_f = last_full.at[kind, :, :, :, features]

        def last_away():
            for way in range(2):
                send(("t1", kind, p, way), block(part, kind, p, across[one], at[two], way),
                     last_h.at[way], device[one][way])

        plan.add(("t1", kind, p), rank, 0.1, [("r", kind, p, 3)], last_away,
                 both(("t1", kind, p), one, size[p] / 2))
        for way in range(2):
            def last_on(way=way):
                arrived(("t1", kind, p, way))
                piece = block(part, kind, p, to[one][way], at[two], way)
                piece[...] = plus(piece, last_h.at[way])
                send(("t2", kind, p, way), block(part, kind, p, to[one][way], at[two]),
                     last_f.at[way], device[one][way])

            plan.add(("t2t", kind, p, way), rank, cost / 2,
                     [("r", kind, p, 2 - way), ("t1", kind, p, way)], last_on,
                     [(("t2", kind, p, way), one + "+-"[way], size[p])])

        def last_sum():
            for way in range(2):
                arrived(("t2", kind, p, way))
            total[kind, :, :, features] = plus(
                block(part, kind, p, at[one], at[two]), last_f.at[0], last_f.at[1])

        plan.add(("t", kind, p), rank, cost,
                 [("r", kind, p, 0), ("t2", kind, p, 0), ("t2", kind, p, 1)], last_sum)

    def chunk_rows(kind, c, e):
        return rows[kind, chunk["z"][c], :, e].reshape(RING * count, depth)

    def place(c):
        return pl.ds(pl.multiple_of(chunk["z"][c] * (RING * count), RING * count), RING * count)

    def forward(c, e):
        pre = lax.dot_general(chunk_rows(0, c, e), w_in[e], (((1,), (1,)), ((), ())),
                              preferred_element_type=F32)
        cdf = normal_cdf(pre)
        act = (pre * cdf).astype(BF16)
        slope[e, place(c)] = cdf + pre * jnp.exp(-0.5 * pre * pre) * 0.3989422804014327
        hidden[e, place(c)] = act
        out = jnp.dot(act, w_out[e], preferred_element_type=F32)
        part[0, chunk["z"][c], :, e] = out.astype(BF16).reshape(RING, count, depth)

    def backward(c, e):
        grad = lax.dot_general(chunk_rows(1, c, e), w_out[e], (((1,), (1,)), ((), ())),
                               preferred_element_type=F32)
        grad = (grad * slope[e, place(c)]).astype(BF16)
        pre_grad[e, place(c)] = grad
        out = jnp.dot(grad, w_in[e], preferred_element_type=F32)
        part[1, chunk["z"][c], :, e] = out.astype(BF16).reshape(RING, count, depth)

    def weight_grad(left, kind, e, target):
        right = rows[kind, :, :, e].reshape(RING * RING * count, depth)
        target[e] = lax.dot_general(left[e], right, (((0,), (0,)), ((), ())),
                                    preferred_element_type=F32).astype(BF16)

    stores = (
        pltpu.make_async_copy(w_in_grad, w_in_grad_ref, store_sem.at[0]),
        pltpu.make_async_copy(w_out_grad, w_out_grad_ref, store_sem.at[1]),
    )

    def begin():
        pl.semaphore_wait(barrier, 4 + group - 1)

    def swap_in(kind):
        if kind == 0:
            make_slots(0)
            begin()
            swap_start(0, 0, outbox, inbox)
        else:
            make_slots(1)
            swap_start(1, 0, outbox, inbox)

    swap_size = 0.17
    for kind in range(2):
        plan.add(("make", kind), -2, 2.0, [("make", 0)] if kind else [], lambda kind=kind: swap_in(kind),
                 [(("swap", kind), "y", swap_size)])
        plan.add(("own", kind), -1, 0.5, [("swap", kind)], lambda kind=kind: own_rows(kind))
        for p in range(2):
            gather(kind, p)
            reduce(kind, p)

    def load_weights():
        loads[2].wait()
        loads[3].wait()

    plan.add("weights", 50, 0.1, [("own", 1)], load_weights)
    for c in range(RING):
        for e in range(members):
            plan.add(("part", 0, c, e), 80, 0.8,
                     ["weights", ("g", 0, 0, c)] + [("g", 0, 1, x) for x in range(RING)],
                     lambda c=c, e=e: forward(c, e))
            plan.add(("part", 1, c, e), 81, 0.8,
                     [("part", 0, c, e), ("g", 1, 0, c)] + [("g", 1, 1, x) for x in range(RING)],
                     lambda c=c, e=e: backward(c, e))
    for kind in range(2):
        plan.add(("back", kind), 60, 0.5, [("t", kind, 0), ("t", kind, 1)],
                 lambda kind=kind: send_back(kind), [(("home", kind), "y", swap_size)])
        plan.add(("finish", kind), 70, 1.0, [("home", kind)] + ([("finish", 0)] if kind else []),
                 lambda kind=kind: finish(kind))
        for e in range(members):
            left, target = ((pre_grad, w_in_grad), (hidden, w_out_grad))[kind]
            after = [("part", 1 - kind, c, m) for c in range(RING) for m in range(members)]
            after += [("g", kind, p, c) for p in range(2) for c in range(RING)]
            plan.add(("weight", kind, e), 100 - kind, 1.2, after,
                     lambda left=left, kind=kind, e=e, target=target: weight_grad(left, kind, e, target))
        plan.add(("store", kind), 90, 0.1, [("weight", kind, e) for e in range(members)],
                 lambda kind=kind: stores[kind].start())

    for _, _, run in plan.order():
        run()

    for copy in sent:
        copy.wait_send()

    def swapped(by, carry):
        for kind in range(2):
            swap_copy(kind, 0, by, outbox, inbox).wait_send()
            swap_copy(kind, 1, by, back_outbox, back_inbox).wait_send()
        return carry

    lax.fori_loop(1, group, swapped, 0)
    for store in stores:
        store.wait()


COPIES = 2 * 2 * 2 * (4 + 4 * RING)


def shards(tokens, logits, out_grad, w_in, w_out):
    images, length, depth = tokens.shape
    slots = logits.shape[2]
    members, width, _ = w_in.shape
    group = slots // members
    count = group * images
    block = (members, count)
    kept = (members, RING * RING * count, width)
    columns = depth // 2 // TILE
    swapped = (2, group, (columns + columns % 2) * 8, TILE)
    split = (SPLIT, depth - SPLIT)
    shape = jax.ShapeDtypeStruct
    whole = pl.BlockSpec(memory_space=pl.ANY)
    inside = pl.BlockSpec(memory_space=pltpu.VMEM)
    return pl.pallas_call(
        kernel,
        out_shape=(
            shape(tokens.shape, BF16),
            shape(logits.shape, F32),
            shape(w_in.shape, BF16),
            shape(w_out.shape, BF16),
        ),
        in_specs=[whole, inside, whole, whole, whole],
        out_specs=(inside, inside, whole, whole),
        scratch_shapes=[
            pltpu.VMEM(tokens.shape, BF16),
            pltpu.VMEM(tokens.shape, BF16),
            pltpu.VMEM(logits.shape, F32),
            pltpu.VMEM(logits.shape, F32),
            pltpu.VMEM(swapped, BF16),
            pltpu.VMEM(swapped, BF16),
            pltpu.VMEM(swapped, BF16),
            pltpu.VMEM(swapped, BF16),
            pltpu.VMEM((2, RING, RING) + block + (depth,), BF16),
            pltpu.VMEM((2, RING, RING) + block + (depth,), BF16),
            pltpu.VMEM((2, RING, 2, count, split[0]), BF16),
            pltpu.VMEM((2, RING, 2) + block + (split[0],), BF16),
            pltpu.VMEM((2, RING, 2, count, split[1]), BF16),
            pltpu.VMEM((2, RING, 2) + block + (split[1],), BF16),
            pltpu.VMEM((2, 2, count, depth), BF16),
            pltpu.VMEM((2, 2) + block + (depth,), BF16),
            pltpu.VMEM((2,) + block + (depth,), BF16),
            pltpu.VMEM(w_in.shape, BF16),
            pltpu.VMEM(w_out.shape, BF16),
            pltpu.VMEM(kept, F32),
            pltpu.VMEM(kept, BF16),
            pltpu.VMEM(kept, BF16),
            pltpu.VMEM(w_in.shape, BF16),
            pltpu.VMEM(w_out.shape, BF16),
            pltpu.SemaphoreType.DMA((4,)),
            pltpu.SemaphoreType.DMA((2,)),
            pltpu.SemaphoreType.DMA((2, 2, group)),
            pltpu.SemaphoreType.DMA((2, 2, group)),
            pltpu.SemaphoreType.DMA((COPIES,)),
            pltpu.SemaphoreType.DMA((COPIES,)),
        ],
        compiler_params=pltpu.CompilerParams(
            collective_id=0, has_side_effects=True, vmem_limit_bytes=56 * 2**20
        ),
    )(tokens, logits, out_grad, w_in, w_out)


def solution(mesh):
    placed = (
        P(("dp", "expert"), None, None),
        P(("dp", "expert"), None, None),
        P(("dp", "expert"), None, None),
        P("expert", "dp", None),
        P("expert", "dp", None),
    )
    return jax.shard_map(
        shards,
        mesh=mesh,
        in_specs=placed,
        out_specs=(
            P(("dp", "expert"), None, None),
            P(("dp", "expert"), None, None),
            P("expert", "dp", None),
            P("expert", "dp", None),
        ),
        check_vma=False,
    )
```

```python
import jax
import jax.numpy as jnp
from jax import lax
from jax.experimental import pallas as pl
from jax.experimental.pallas import tpu as pltpu
from jax.sharding import PartitionSpec as P

RING = 4
TILE = 128
SPLIT = 1024
MESH = pl.DeviceIdType.MESH
BF16 = jnp.bfloat16
F32 = jnp.float32


def normal_cdf(values):
    return 0.5 * (1.0 + lax.erf(values * 0.7071067811865476))


def soft_weights(values, over_dim):
    highest = jnp.max(values, axis=over_dim, keepdims=True)
    raised = jnp.exp(values - highest)
    return raised / jnp.sum(raised, axis=over_dim, keepdims=True)


def shift(at, by, size):
    return lax.rem(at + (by + size), size)


def iota(shape, dim):
    return lax.broadcasted_iota(jnp.int32, shape, dim)


def zero_one(mask):
    return mask.astype(F32).astype(BF16)


def tiled(block, group):
    packed, features = block.shape
    pieces = [
        block[:, at * TILE:(at + 1) * TILE].reshape(group, 1, packed // group, TILE)
        for at in range(features // TILE)
    ]
    if len(pieces) % 2:
        pieces.append(jnp.zeros_like(pieces[0]))
    block = jnp.concatenate(pieces, axis=1)
    return block.reshape(group, len(pieces) * (packed // group), TILE).astype(BF16)


def untiled(block, features):
    group, high, _ = block.shape
    block = block.astype(F32).reshape(group, high // 8, 8, TILE)
    return jnp.concatenate(
        [block[:, at].reshape(group * 8, TILE) for at in range(features // TILE)], axis=1
    ).astype(BF16)


def picker(packed, half, by_member):
    shape = (packed // 2, packed)
    row, column = iota(shape, 0), iota(shape, 1)
    first, source, second = row // (packed // 4), (row % (packed // 4)) // 2, row % 2
    image, member = (second, first) if by_member else (first, second)
    return zero_one(column == ((source * 2 + half) * 2 + image) * 2 + member)


def unpack(block, depth, by_member):
    block = untiled(block, depth // 2)
    return jnp.concatenate(
        [jnp.dot(picker(block.shape[0], half, by_member), block, preferred_element_type=F32)
         for half in range(2)],
        axis=1,
    ).astype(BF16)


def pack(block):
    rows, depth = block.shape
    return sum(
        lax.dot_general(picker(2 * rows, half, True), block[:, half * depth // 2:(half + 1) * depth // 2],
                        (((0,), (0,)), ((), ())), preferred_element_type=F32)
        for half in range(2)
    )


ORDER = (
    ("make", 0), ("make", 1), ("own", 0), ("g1", 0, 0), ("s1", 0, 0, 0), ("g1", 0, 1), ("own", 1), ("g1", 1, 1),
    ("weights",), ("s1", 1, 0, 0), ("g1", 1, 0), ("s2t", 0, 0, 0, 0), ("s2t", 0, 0, 0, 1), ("g2t", 0, 1, 0),
    ("g2t", 1, 1, 1), ("g2t", 0, 1, 1), ("g2t", 1, 1, 0), ("s2t", 1, 0, 0, 0), ("s2t", 1, 0, 0, 1),
    ("g2t", 0, 0, 1), ("g2t", 0, 0, 0), ("s1", 0, 0, 2), ("g", 0, 0, 0), ("s1", 0, 0, 1), ("s1", 0, 1, 2),
    ("g", 1, 0, 0), ("s1", 0, 1, 1), ("s1", 0, 1, 0), ("s2t", 0, 0, 2, 0), ("s2t", 0, 0, 2, 1), ("s1", 0, 0, 3),
    ("s1", 0, 1, 3), ("s2t", 0, 1, 2, 0), ("g2t", 1, 0, 1), ("g2t", 1, 0, 0), ("s2t", 0, 0, 1, 0),
    ("s2t", 0, 0, 1, 1), ("g", 0, 0, 2), ("s1", 1, 0, 2), ("s2t", 0, 1, 1, 1), ("s2t", 0, 1, 1, 0),
    ("s2t", 0, 1, 0, 1), ("s2t", 0, 1, 0, 0), ("s2t", 0, 1, 3, 1), ("s2t", 0, 1, 3, 0), ("s2t", 0, 0, 3, 0),
    ("s2t", 0, 0, 3, 1), ("s1", 1, 1, 2), ("g", 0, 0, 1), ("s2t", 0, 1, 2, 1), ("s1", 1, 0, 1), ("s1", 1, 1, 3),
    ("g", 0, 1, 1), ("s1", 1, 1, 1), ("g", 0, 1, 0), ("s2t", 1, 0, 2, 0), ("s2t", 1, 0, 2, 1), ("g", 0, 1, 3),
    ("s1", 1, 1, 0), ("g", 0, 0, 3), ("s1", 1, 0, 3), ("g", 0, 1, 2), ("part", 0, 3, 1), ("part", 0, 3, 0),
    ("part", 0, 0, 1), ("part", 0, 1, 1), ("s2t", 1, 0, 1, 0), ("s2t", 1, 0, 1, 1), ("part", 0, 2, 0),
    ("s2t", 1, 1, 1, 1), ("s2t", 1, 1, 1, 0), ("s2t", 1, 1, 3, 1), ("s2t", 1, 1, 3, 0), ("s2t", 1, 1, 2, 0),
    ("r1", 0, 0, 3), ("part", 0, 0, 0), ("s2t", 1, 1, 0, 1), ("s2t", 1, 1, 2, 1), ("s2t", 1, 1, 0, 0),
    ("part", 0, 2, 1), ("r1", 0, 0, 2), ("part", 0, 1, 0), ("r1", 0, 1, 0), ("s2t", 1, 0, 3, 1),
    ("r1", 0, 0, 1), ("r1", 0, 1, 1), ("g", 1, 1, 1), ("r1", 0, 1, 3), ("r1", 0, 1, 2), ("g", 1, 1, 3),
    ("g", 1, 0, 2), ("g", 1, 0, 1), ("s2t", 1, 0, 3, 0), ("g", 1, 1, 2), ("g", 1, 1, 0), ("part", 1, 1, 1),
    ("part", 1, 2, 0), ("r2t", 0, 0, 3, 0), ("r2t", 0, 1, 1, 1), ("r2t", 0, 0, 3, 1), ("r2t", 0, 1, 0, 0),
    ("r2t", 0, 1, 1, 0), ("r2t", 0, 1, 0, 1), ("part", 1, 2, 1), ("r2t", 0, 1, 3, 1), ("part", 1, 0, 0),
    ("r2t", 0, 1, 2, 0), ("part", 1, 0, 1), ("r2t", 0, 0, 2, 0), ("r2t", 0, 0, 2, 1), ("r2t", 0, 1, 3, 0),
    ("r2t", 0, 1, 2, 1), ("part", 1, 1, 0), ("g", 1, 0, 3), ("weight", 1, 0), ("part", 1, 3, 1),
    ("part", 1, 3, 0), ("r1", 1, 0, 3), ("r", 0, 1, 1), ("r1", 1, 1, 0), ("r1", 1, 1, 1), ("weight", 0, 0),
    ("r2t", 0, 0, 1, 1), ("r2t", 0, 0, 1, 0), ("r", 0, 0, 3), ("t1", 0, 0), ("weight", 0, 1), ("store", 0),
    ("r", 0, 1, 2), ("r", 0, 1, 0), ("weight", 1, 1), ("r", 0, 1, 3), ("store", 1), ("r2t", 1, 1, 0, 1),
    ("r1", 1, 1, 3), ("r2t", 1, 1, 0, 0), ("r", 0, 0, 2), ("r1", 1, 0, 1), ("r2t", 1, 1, 1, 1), ("r1", 1, 1, 2),
    ("r2t", 1, 0, 3, 0), ("r2t", 1, 0, 3, 1), ("r2t", 1, 1, 1, 0), ("t2t", 0, 0, 0), ("r", 0, 0, 1),
    ("r1", 1, 0, 2), ("t2t", 0, 0, 1), ("r", 1, 1, 0), ("r2t", 1, 0, 1, 0), ("r2t", 1, 0, 1, 1), ("r", 1, 1, 1),
    ("r", 1, 0, 3), ("r1", 0, 0, 0), ("t1", 1, 0), ("r2t", 1, 0, 2, 0), ("r2t", 1, 0, 2, 1),
    ("r2t", 1, 1, 3, 1), ("r2t", 1, 1, 3, 0), ("r", 1, 0, 1), ("t1", 0, 1), ("r2t", 1, 1, 2, 1),
    ("r1", 1, 0, 0), ("r2t", 1, 1, 2, 0), ("r2t", 0, 0, 0, 0), ("r2t", 0, 0, 0, 1), ("t2t", 1, 0, 1),
    ("r", 1, 0, 2), ("t2t", 1, 0, 0), ("r", 1, 1, 3), ("t2t", 0, 1, 0), ("t1", 1, 1), ("t2t", 0, 1, 1),
    ("r2t", 1, 0, 0, 0), ("r2t", 1, 0, 0, 1), ("r", 1, 1, 2), ("r", 0, 0, 0), ("t", 0, 0), ("t2t", 1, 1, 1),
    ("t2t", 1, 1, 0), ("t", 0, 1), ("back", 0), ("r", 1, 0, 0), ("t", 1, 0), ("t", 1, 1), ("back", 1),
    ("finish", 0), ("finish", 1),
)


def kernel(
    tokens, logits_ref, out_grad, w_in_ref, w_out_ref,
    slot_in_grad_ref, from_combine_ref, w_in_grad_ref, w_out_grad_ref,
    combine, outbox, inbox, back_outbox, back_inbox,
    rows, part, half_a, full_a, half_b, full_b, last_half, last_full, total,
    w_in, w_out, slope, hidden, pre_grad, w_in_grad, w_out_grad,
    load_sem, store_sem, swap_send, swap_recv, send_sem, recv_sem,
):
    members, count, depth = rows.shape[3:]
    images, slots, length = combine.shape
    group = slots // members
    packed = group * 2 * images * members
    me = lax.axis_index("dp")
    mine = lax.axis_index("expert")
    at = {"z": me // RING, "x": lax.rem(me, RING)}
    to = {axis: (shift(at[axis], 1, RING), shift(at[axis], -1, RING)) for axis in "zx"}
    come = {axis: (to[axis][1], to[axis][0]) for axis in "zx"}
    across = {axis: shift(at[axis], 2, RING) for axis in "zx"}
    device = {
        "z": tuple(z * RING + at["x"] for z in to["z"]),
        "x": tuple(at["z"] * RING + x for x in to["x"]),
    }
    chunk = {axis: (at[axis], come[axis][0], come[axis][1], across[axis]) for axis in "zx"}
    halves = (
        ("z", "x", pl.ds(0, SPLIT)),
        ("x", "z", pl.ds(SPLIT, depth - SPLIT)),
    )
    width = (SPLIT, depth - SPLIT)
    half_buf, full_buf = (half_a, half_b), (full_a, full_b)

    def partner(by):
        return lax.rem(mine + by, group)

    barrier = pltpu.get_barrier_semaphore()
    for axis in "zx":
        for there in device[axis]:
            pl.semaphore_signal(barrier, inc=1, device_id={"dp": there}, device_id_type=MESH)

    def greet(by, carry):
        pl.semaphore_signal(barrier, inc=1, device_id={"expert": partner(by)}, device_id_type=MESH)
        return carry

    lax.fori_loop(1, group, greet, 0)

    loads = [
        pltpu.make_async_copy(source, target, load_sem.at[i])
        for i, (source, target) in enumerate(
            ((w_in_ref, w_in), (w_out_ref, w_out))
        )
    ]
    for load in loads:
        load.start()

    def swap_copy(kind, way, by, box, inbound):
        return pltpu.make_async_remote_copy(
            src_ref=box.at[kind, partner(by)], dst_ref=inbound.at[kind, mine],
            send_sem=swap_send.at[way, kind, by], recv_sem=swap_recv.at[way, kind, by],
            device_id={"expert": partner(by)}, device_id_type=MESH,
        )

    def swap_start(kind, way, box, inbound):
        def one(by, carry):
            swap_copy(kind, way, by, box, inbound).start()
            return carry

        lax.fori_loop(1, group, one, 0)
        inbound[kind, mine] = box[kind, mine]

    def swap_arrived(kind, way, box, inbound):
        def one(by, carry):
            swap_copy(kind, way, by, box, inbound).wait_recv()
            return carry

        lax.fori_loop(1, group, one, 0)

    def make_slots(kind):
        source = (tokens, out_grad)[kind]
        left = []
        for image in range(images):
            soft = soft_weights(logits_ref[image], 1 - kind)
            if kind == 1:
                combine[image] = soft
            row, slot = iota((packed, slots), 0), iota((packed, slots), 1)
            spread = zero_one((slot == (row // 8) * 2 + row % 2) & ((row // 2) % 2 == image))
            left.append(jnp.dot(spread, soft.astype(BF16), preferred_element_type=F32).astype(BF16))
        slot = jnp.dot(jnp.concatenate(left, axis=1), source[...].reshape(images * length, depth),
                       preferred_element_type=F32)
        first = (iota((packed, depth // 2), 0) // 4) % 2 == 0
        outbox[kind] = tiled(jnp.where(first, slot[:, :depth // 2], slot[:, depth // 2:]), group)

    def own_rows(kind):
        swap_arrived(kind, 0, outbox, inbox)
        rows[kind, at["z"], at["x"]] = unpack(inbox[kind], depth, True).reshape(members, count, depth)

    def send_back(kind):
        back_outbox[kind] = tiled(pack(total[kind].reshape(members * count, depth)), group)
        swap_start(kind, 1, back_outbox, back_inbox)

    def finish(kind):
        swap_arrived(kind, 1, back_outbox, back_inbox)
        back = unpack(back_inbox[kind], depth, False)
        if kind == 1:
            slot_in_grad_ref[...] = back
            return
        for image in range(images):
            grad = lax.dot_general(back[image * slots:(image + 1) * slots], out_grad[image],
                                   (((1,), (1,)), ((), ())), preferred_element_type=F32)
            soft = combine[image]
            from_combine_ref[image] = soft * (grad - jnp.sum(soft * grad, axis=0, keepdims=True))

    sent = []
    flying = {}

    def send(key, source, target, there):
        copy = pltpu.make_async_remote_copy(
            src_ref=source, dst_ref=target,
            send_sem=send_sem.at[len(sent)], recv_sem=recv_sem.at[len(sent)],
            device_id={"dp": there}, device_id_type=MESH,
        )
        copy.start()
        sent.append(copy)
        flying[key] = copy

    def arrived(key):
        flying.pop(key).wait_recv()

    def block(ref, kind, p, first, second, member=None):
        z, x = (first, second) if halves[p][0] == "z" else (second, first)
        return ref.at[kind, z, x, slice(None) if member is None else member, :, halves[p][2]]

    tasks = {}

    def gather(kind, p):
        one, two, _ = halves[p]

        def along_one():
            mine_here = block(rows, kind, p, at[one], at[two])
            for way in range(2):
                send(("g1", kind, p, way), mine_here, mine_here, device[one][way])

        tasks["g1", kind, p] = along_one
        for way in range(2):
            def on_one(way=way):
                arrived(("g1", kind, p, way))
                piece = block(rows, kind, p, come[one][way], at[two], way)
                send(("g2", kind, p, way), piece, piece, device[one][way])

            tasks["g2t", kind, p, way] = on_one

        for c in range(RING):
            def along_two(c=c):
                if c == 3:
                    for way in range(2):
                        arrived(("g2", kind, p, way))
                here = block(rows, kind, p, chunk[one][c], at[two])
                for way in range(2):
                    send(("s1", kind, p, c, way), here, here, device[two][way])

            tasks["s1", kind, p, c] = along_two
            for way in range(2):
                def on_two(c=c, way=way):
                    arrived(("s1", kind, p, c, way))
                    piece = block(rows, kind, p, chunk[one][c], come[two][way], way)
                    send(("s2", kind, p, c, way), piece, piece, device[two][way])

                tasks["s2t", kind, p, c, way] = on_two

            def gathered(c=c):
                for way in range(2):
                    arrived(("s2", kind, p, c, way))

            tasks["g", kind, p, c] = gathered

    def plus(*refs):
        value = refs[0][...].astype(F32)
        for ref in refs[1:]:
            value = value + ref[...].astype(F32)
        return value.astype(BF16)

    def reduce(kind, p):
        one, two, features = halves[p]
        half_in, full_in = half_buf[p], full_buf[p]
        for c in range(RING):
            def away(c=c):
                for way in range(2):
                    send(("r1", kind, p, c, way),
                         block(part, kind, p, chunk[one][c], across[two], way),
                         half_in.at[kind, c, way], device[two][way])

            tasks["r1", kind, p, c] = away
            for way in range(2):
                def add_on(c=c, way=way):
                    arrived(("r1", kind, p, c, way))
                    piece = block(part, kind, p, chunk[one][c], to[two][way], way)
                    piece[...] = plus(piece, half_in.at[kind, c, way])
                    send(("r2", kind, p, c, way), block(part, kind, p, chunk[one][c], to[two][way]),
                         full_in.at[kind, c, way], device[two][way])

                tasks["r2t", kind, p, c, way] = add_on

            def summed(c=c):
                for way in range(2):
                    arrived(("r2", kind, p, c, way))
                here = block(part, kind, p, chunk[one][c], at[two])
                here[...] = plus(here, full_in.at[kind, c, 0], full_in.at[kind, c, 1])

            tasks["r", kind, p, c] = summed

        last_h = last_half.at[kind, :, :, features]
        last_f = last_full.at[kind, :, :, :, features]

        def last_away():
            for way in range(2):
                send(("t1", kind, p, way), block(part, kind, p, across[one], at[two], way),
                     last_h.at[way], device[one][way])

        tasks["t1", kind, p] = last_away
        for way in range(2):
            def last_on(way=way):
                arrived(("t1", kind, p, way))
                piece = block(part, kind, p, to[one][way], at[two], way)
                piece[...] = plus(piece, last_h.at[way])
                send(("t2", kind, p, way), block(part, kind, p, to[one][way], at[two]),
                     last_f.at[way], device[one][way])

            tasks["t2t", kind, p, way] = last_on

        def last_sum():
            for way in range(2):
                arrived(("t2", kind, p, way))
            total[kind, :, :, features] = plus(
                block(part, kind, p, at[one], at[two]), last_f.at[0], last_f.at[1])

        tasks["t", kind, p] = last_sum

    def chunk_rows(kind, c, e):
        return rows[kind, chunk["z"][c], :, e].reshape(RING * count, depth)

    def place(c):
        return pl.ds(pl.multiple_of(chunk["z"][c] * (RING * count), RING * count), RING * count)

    def forward(c, e):
        pre = lax.dot_general(chunk_rows(0, c, e), w_in[e], (((1,), (1,)), ((), ())),
                              preferred_element_type=F32)
        cdf = normal_cdf(pre)
        act = (pre * cdf).astype(BF16)
        slope[e, place(c)] = cdf + pre * jnp.exp(-0.5 * pre * pre) * 0.3989422804014327
        hidden[e, place(c)] = act
        out = jnp.dot(act, w_out[e], preferred_element_type=F32)
        part[0, chunk["z"][c], :, e] = out.astype(BF16).reshape(RING, count, depth)

    def backward(c, e):
        grad = lax.dot_general(chunk_rows(1, c, e), w_out[e], (((1,), (1,)), ((), ())),
                               preferred_element_type=F32)
        grad = (grad * slope[e, place(c)]).astype(BF16)
        pre_grad[e, place(c)] = grad
        out = jnp.dot(grad, w_in[e], preferred_element_type=F32)
        part[1, chunk["z"][c], :, e] = out.astype(BF16).reshape(RING, count, depth)

    def weight_grad(left, kind, e, target):
        right = rows[kind, :, :, e].reshape(RING * RING * count, depth)
        target[e] = lax.dot_general(left[e], right, (((0,), (0,)), ((), ())),
                                    preferred_element_type=F32).astype(BF16)

    stores = (
        pltpu.make_async_copy(w_in_grad, w_in_grad_ref, store_sem.at[0]),
        pltpu.make_async_copy(w_out_grad, w_out_grad_ref, store_sem.at[1]),
    )

    def swap_in(kind):
        make_slots(kind)
        if kind == 0:
            pl.semaphore_wait(barrier, 4 + group - 1)
        swap_start(kind, 0, outbox, inbox)

    def load_weights():
        for load in loads:
            load.wait()

    tasks["weights",] = load_weights
    for kind in range(2):
        tasks["make", kind] = lambda kind=kind: swap_in(kind)
        tasks["own", kind] = lambda kind=kind: own_rows(kind)
        for p in range(2):
            gather(kind, p)
            reduce(kind, p)
        for c in range(RING):
            for e in range(members):
                tasks["part", kind, c, e] = lambda kind=kind, c=c, e=e: (forward, backward)[kind](c, e)
        tasks["back", kind] = lambda kind=kind: send_back(kind)
        tasks["finish", kind] = lambda kind=kind: finish(kind)
        left, target = ((pre_grad, w_in_grad), (hidden, w_out_grad))[kind]
        for e in range(members):
            tasks["weight", kind, e] = (
                lambda left=left, kind=kind, e=e, target=target: weight_grad(left, kind, e, target))
        tasks["store", kind] = lambda kind=kind: stores[kind].start()

    assert sorted(tasks, key=str) == sorted(ORDER, key=str)
    for name in ORDER:
        tasks[name]()

    for copy in sent:
        copy.wait_send()

    def swapped(by, carry):
        for kind in range(2):
            swap_copy(kind, 0, by, outbox, inbox).wait_send()
            swap_copy(kind, 1, by, back_outbox, back_inbox).wait_send()
        return carry

    lax.fori_loop(1, group, swapped, 0)
    for store in stores:
        store.wait()


def last_kernel(
    tokens, logits_ref, slot_in_grad_ref, from_combine_ref, w_in_grad_ref, w_out_grad_ref,
    token_grad_ref, logit_grad_ref, w_in_out_ref, w_out_out_ref,
    token_grad, sem, token_sem,
):
    images, slots, _ = logits_ref.shape
    moves = [
        pltpu.make_async_copy(source.at[e], target.at[e], sem.at[2 * i + e])
        for i, (source, target) in enumerate(
            ((w_in_grad_ref, w_in_out_ref), (w_out_grad_ref, w_out_out_ref)))
        for e in range(2)
    ]
    for move in moves:
        move.start()
    softs = []
    for image in range(images):
        back = slot_in_grad_ref[image * slots:(image + 1) * slots]
        softs.append(soft_weights(logits_ref[image], 1))
        token_grad[image] = lax.dot_general(
            softs[image].astype(BF16), back, (((0,), (0,)), ((), ())), preferred_element_type=F32
        ).astype(BF16)
        moves.append(pltpu.make_async_copy(token_grad.at[image], token_grad_ref.at[image], token_sem.at[image]))
        moves[-1].start()
    for image in range(images):
        back = slot_in_grad_ref[image * slots:(image + 1) * slots]
        grad = lax.dot_general(back, tokens[image], (((1,), (1,)), ((), ())), preferred_element_type=F32)
        soft = softs[image]
        grad = soft * (grad - jnp.sum(soft * grad, axis=1, keepdims=True))
        logit_grad_ref[image] = from_combine_ref[image] + grad
    for move in moves:
        move.wait()


COPIES = 2 * 2 * 2 * (4 + 4 * RING)


def shards(tokens, logits, out_grad, w_in, w_out):
    images, length, depth = tokens.shape
    slots = logits.shape[2]
    logits = jnp.transpose(logits, (0, 2, 1))
    members, width, _ = w_in.shape
    group = slots // members
    count = group * images
    block = (members, count)
    kept = (members, RING * RING * count, width)
    columns = depth // 2 // TILE
    swapped = (2, group, (columns + columns % 2) * 8, TILE)
    split = (SPLIT, depth - SPLIT)
    shape = jax.ShapeDtypeStruct
    whole = pl.BlockSpec(memory_space=pl.ANY)
    inside = pl.BlockSpec(memory_space=pltpu.VMEM)
    far = pl.BlockSpec(memory_space=pltpu.HBM)
    slot_in_grad, from_combine, w_in_grad, w_out_grad = pl.pallas_call(
        kernel,
        out_shape=(
            shape((images * slots, depth), BF16),
            shape(logits.shape, F32),
            shape(w_in.shape, BF16),
            shape(w_out.shape, BF16),
        ),
        in_specs=[inside, inside, inside, far, far],
        out_specs=(inside, inside, whole, whole),
        scratch_shapes=[
            pltpu.VMEM(logits.shape, F32),
            pltpu.VMEM(swapped, BF16),
            pltpu.VMEM(swapped, BF16),
            pltpu.VMEM(swapped, BF16),
            pltpu.VMEM(swapped, BF16),
            pltpu.VMEM((2, RING, RING) + block + (depth,), BF16),
            pltpu.VMEM((2, RING, RING) + block + (depth,), BF16),
            pltpu.VMEM((2, RING, 2, count, split[0]), BF16),
            pltpu.VMEM((2, RING, 2) + block + (split[0],), BF16),
            pltpu.VMEM((2, RING, 2, count, split[1]), BF16),
            pltpu.VMEM((2, RING, 2) + block + (split[1],), BF16),
            pltpu.VMEM((2, 2, count, depth), BF16),
            pltpu.VMEM((2, 2) + block + (depth,), BF16),
            pltpu.VMEM((2,) + block + (depth,), BF16),
            pltpu.VMEM(w_in.shape, BF16),
            pltpu.VMEM(w_out.shape, BF16),
            pltpu.VMEM(kept, F32),
            pltpu.VMEM(kept, BF16),
            pltpu.VMEM(kept, BF16),
            pltpu.VMEM(w_in.shape, BF16),
            pltpu.VMEM(w_out.shape, BF16),
            pltpu.SemaphoreType.DMA((2,)),
            pltpu.SemaphoreType.DMA((2,)),
            pltpu.SemaphoreType.DMA((2, 2, group)),
            pltpu.SemaphoreType.DMA((2, 2, group)),
            pltpu.SemaphoreType.DMA((COPIES,)),
            pltpu.SemaphoreType.DMA((COPIES,)),
        ],
        compiler_params=pltpu.CompilerParams(
            collective_id=0, has_side_effects=True, vmem_limit_bytes=48 * 2**20
        ),
    )(tokens, logits, out_grad, w_in, w_out)
    token_grad, logit_grad, w_in_grad, w_out_grad = pl.pallas_call(
        last_kernel,
        out_shape=(
            shape(tokens.shape, BF16),
            shape(logits.shape, F32),
            shape(w_in.shape, BF16),
            shape(w_out.shape, BF16),
        ),
        in_specs=[inside, inside, inside, inside, whole, whole],
        out_specs=(whole, inside, whole, whole),
        scratch_shapes=[
            pltpu.VMEM(tokens.shape, BF16),
            pltpu.SemaphoreType.DMA((4,)),
            pltpu.SemaphoreType.DMA((2,)),
        ],
        compiler_params=pltpu.CompilerParams(vmem_limit_bytes=16 * 2**20),
    )(tokens, logits, slot_in_grad, from_combine, w_in_grad, w_out_grad)
    return token_grad, jnp.transpose(logit_grad, (0, 2, 1)), w_in_grad, w_out_grad


def solution(mesh):
    placed = (
        P(("dp", "expert"), None, None),
        P(("dp", "expert"), None, None),
        P(("dp", "expert"), None, None),
        P("expert", "dp", None),
        P("expert", "dp", None),
    )
    return jax.shard_map(
        shards,
        mesh=mesh,
        in_specs=placed,
        out_specs=(
            P(("dp", "expert"), None, None),
            P(("dp", "expert"), None, None),
            P("expert", "dp", None),
            P("expert", "dp", None),
        ),
        check_vma=False,
    )
```

```python
import jax
import jax.numpy as jnp
from jax import lax
from jax.experimental import pallas as pl
from jax.experimental.pallas import tpu as pltpu
from jax.sharding import PartitionSpec as P

RING = 4
TILE = 128
SPLIT = 768
PIECES = 5
COPIES = 2 * 74 + 4 * PIECES
MESH = pl.DeviceIdType.MESH
BF16 = jnp.bfloat16
F32 = jnp.float32


def normal_cdf(values):
    return 0.5 * (1.0 + lax.erf(values * 0.7071067811865476))


def soft_weights(values, over_dim):
    highest = jnp.max(values, axis=over_dim, keepdims=True)
    raised = jnp.exp(values - highest)
    return raised / jnp.sum(raised, axis=over_dim, keepdims=True)


def shift(at, by, size):
    return lax.rem(at + (by + size), size)


def iota(shape, dim):
    return lax.broadcasted_iota(jnp.int32, shape, dim)


def zero_one(mask):
    return mask.astype(F32).astype(BF16)


def tiled(block, group):
    packed, features = block.shape
    pieces = [
        block[:, at * TILE:(at + 1) * TILE].reshape(group, 1, packed // group, TILE)
        for at in range(features // TILE)
    ]
    if len(pieces) % 2:
        pieces.append(jnp.zeros_like(pieces[0]))
    block = jnp.concatenate(pieces, axis=1)
    return block.reshape(group, len(pieces) * (packed // group), TILE).astype(BF16)


def untiled(block, features):
    group, high, _ = block.shape
    block = block.astype(F32).reshape(group, high // 8, 8, TILE)
    return jnp.concatenate(
        [block[:, at].reshape(group * 8, TILE) for at in range(features // TILE)], axis=1
    ).astype(BF16)


def picker(packed, half, by_member, lead):
    shape = (packed // 2, packed)
    row, column = iota(shape, 0), iota(shape, 1)
    first, source, second = row // (packed // 4), (row % (packed // 4)) // 2, row % 2
    image, member = (second, (first + lead) % 2) if by_member else (first, second)
    return zero_one(column == ((source * 2 + half) * 2 + image) * 2 + member)


def unpack(block, depth, by_member, lead=0):
    block = untiled(block, depth // 2)
    return jnp.concatenate(
        [jnp.dot(picker(block.shape[0], half, by_member, lead), block, preferred_element_type=F32)
         for half in range(2)],
        axis=1,
    ).astype(BF16)


def pack(block, lead):
    rows, depth = block.shape
    return sum(
        lax.dot_general(picker(2 * rows, half, True, lead), block[:, half * depth // 2:(half + 1) * depth // 2],
                        (((0,), (0,)), ((), ())), preferred_element_type=F32)
        for half in range(2)
    )


ORDER = (
    ("enter",), ("make", 0), ("ws", 3), ("ws", 2), ("make", 1), ("ws", 0), ("ws", 8), ("own", 0), ("z1", 0, 0),
    ("g1", 0), ("b1", 0), ("ws", 9), ("own", 1), ("b1", 1), ("ws", 6), ("z1", 1, 0), ("b2t", 0), ("z1", 0, 1),
    ("ws", 5), ("z2t", 0, 0, 0), ("z1", 0, 2), ("ws", 4), ("g2t", 0, 1), ("g2t", 0, 0), ("ws", 7), ("z1", 0, 3),
    ("s1", 0, 0), ("z2t", 1, 0, 1), ("s1", 0, 2), ("z2t", 0, 1, 0), ("z2t", 0, 2, 1), ("s1", 0, 1),
    ("z2t", 1, 0, 0), ("z2t", 0, 1, 1), ("z2t", 0, 2, 0), ("z1", 1, 2), ("ws", 1), ("z2t", 0, 3, 1),
    ("s2t", 0, 0), ("z2t", 0, 3, 0), ("z2t", 0, 0, 1), ("s1", 0, 3), ("g1", 1), ("zg", 0, 1), ("zg", 1, 0),
    ("s2t", 0, 2), ("zg", 0, 2), ("s2t", 0, 1), ("b2t", 1), ("s1", 1, 0), ("weights",), ("g", 0, 0),
    ("zg", 0, 3), ("zg", 0, 0), ("part", 0, 0), ("z2t", 1, 2, 1), ("z2t", 1, 2, 0), ("z1", 1, 1), ("s2t", 0, 3),
    ("r1", 0, 0), ("g", 0, 1), ("part", 0, 1), ("r1", 0, 1), ("z1", 1, 3), ("s2t", 1, 0), ("g", 0, 2),
    ("part", 0, 2), ("zg", 1, 2), ("g2t", 1, 1), ("g2t", 1, 0), ("r2t", 0, 0), ("s1", 1, 2), ("g", 0, 3),
    ("part", 0, 3), ("z2t", 1, 1, 1), ("r2t", 0, 1), ("q1", 0, 1), ("q1", 0, 0), ("r1", 0, 3), ("r1", 0, 2),
    ("g", 1, 0), ("z2t", 1, 1, 0), ("r", 0, 0), ("s1", 1, 1), ("z2t", 1, 3, 1), ("z2t", 1, 3, 0), ("q1", 0, 3),
    ("s2t", 1, 2), ("r", 0, 1), ("q1", 0, 2), ("s1", 1, 3), ("q2t", 0, 1, 0), ("r2t", 0, 3), ("q2t", 0, 1, 1),
    ("r2t", 0, 2), ("zg", 1, 1), ("q2t", 0, 0, 0), ("q2t", 0, 0, 1), ("zg", 1, 3), ("part", 1, 0),
    ("s2t", 1, 1), ("q2t", 0, 3, 0), ("q2t", 0, 3, 1), ("g", 1, 2), ("part", 1, 2), ("s2t", 1, 3), ("r", 0, 3),
    ("q", 0, 1), ("q2t", 0, 2, 0), ("r1", 1, 2), ("q2t", 0, 2, 1), ("r1", 1, 0), ("t1", 0), ("r", 0, 2),
    ("g", 1, 1), ("part", 1, 1), ("r1", 1, 1), ("q", 0, 0), ("g", 1, 3), ("part", 1, 3), ("q1", 1, 2),
    ("r1", 1, 3), ("r2t", 1, 0), ("q", 0, 3), ("q1", 1, 1), ("r2t", 1, 2), ("q1", 1, 3), ("weight", 0),
    ("r2t", 1, 1), ("t2t", 0, 1), ("t2t", 0, 0), ("ds", 0, 2), ("q", 0, 2), ("weight", 1), ("r2t", 1, 3),
    ("v1", 0), ("r", 1, 0), ("r", 1, 2), ("ds", 1, 1), ("r", 1, 1), ("q2t", 1, 3, 1), ("q2t", 1, 3, 0),
    ("ds", 0, 3), ("q2t", 1, 2, 1), ("q2t", 1, 2, 0), ("r", 1, 3), ("t1", 1), ("v2t", 0), ("ds", 1, 2),
    ("t", 0), ("q1", 1, 0), ("q", 1, 3), ("ds", 1, 3), ("q2t", 1, 1, 1), ("q2t", 1, 1, 0), ("q", 1, 2),
    ("v", 0), ("back", 0), ("v1", 1), ("ds", 1, 4), ("t2t", 1, 1), ("t2t", 1, 0), ("ds", 1, 0), ("q", 1, 1),
    ("v2t", 1), ("q2t", 1, 0, 1), ("ds", 0, 0), ("q2t", 1, 0, 0), ("finish", 0), ("ds", 0, 1), ("store", 1),
    ("t", 1), ("ds", 0, 4), ("q", 1, 0), ("v", 1), ("back", 1), ("store", 0), ("finish", 1),
)


def kernel(
    tokens, logits_ref, out_grad, w_in_ref, w_out_ref,
    slot_in_grad_ref, from_combine_ref, w_in_grad_ref, w_out_grad_ref,
    combine, outbox, inbox, back_outbox, back_inbox,
    rows, other, part, other_part, from_twin, last_half, last_full, side_half, side_full, side_twin, total,
    weights, weight_grads, mate_grads, slope, hidden, pre_grad,
    load_sem, store_sem, swap_send, swap_recv, send_sem, recv_sem,
):
    count, depth = rows.shape[3:]
    width = weights.shape[1] // 2
    images, slots, length = combine.shape
    members = 2
    group = slots // members
    packed = group * 2 * images * members
    me = lax.axis_index("dp")
    mine = lax.axis_index("expert")
    z, x = me // RING, lax.rem(me, RING)
    z_to = (shift(z, 1, RING), shift(z, -1, RING))
    z_from = (z_to[1], z_to[0])
    chunk = (z, z_from[0], z_from[1], shift(z, 2, RING))
    z_dev = tuple(to * RING + x for to in z_to)
    turn = lax.rem(mine, 2)
    turned = shift(x, turn, RING)
    mate = shift(turned + 1 - 2 * lax.rem(turned, 2), RING - turn, RING)
    twin = shift(RING - 1 - turned, RING - turn, RING)
    beyond = shift(x, 2, RING)
    places = (x, mate, twin, beyond)
    mate_dev, twin_dev = z * RING + mate, z * RING + twin
    own = lax.rem((turned + 1) // 2, 2)
    first, second = pl.ds(0, SPLIT), pl.ds(SPLIT, depth - SPLIT)
    halves = (pl.ds(0, count // 2), pl.ds(count // 2, count // 2))

    def partner(by):
        return lax.rem(mine + by, group)

    barrier = pltpu.get_barrier_semaphore()
    for there in z_dev + (mate_dev, twin_dev):
        pl.semaphore_signal(barrier, inc=1, device_id={"dp": there}, device_id_type=MESH)

    def greet(by, carry):
        pl.semaphore_signal(barrier, inc=1, device_id={"expert": partner(by)}, device_id_type=MESH)
        return carry

    lax.fori_loop(1, group, greet, 0)

    loads = [
        pltpu.make_async_copy(source.at[own], weights.at[i, pl.ds(0, width)], load_sem.at[i])
        for i, source in enumerate((w_in_ref, w_out_ref))
    ]
    for load in loads:
        load.start()

    def swap_copy(kind, way, by, box, inbound):
        return pltpu.make_async_remote_copy(
            src_ref=box.at[kind, partner(by)], dst_ref=inbound.at[kind, mine],
            send_sem=swap_send.at[way, kind, by], recv_sem=swap_recv.at[way, kind, by],
            device_id={"expert": partner(by)}, device_id_type=MESH,
        )

    def swap_start(kind, way, box, inbound):
        def one(by, carry):
            swap_copy(kind, way, by, box, inbound).start()
            return carry

        lax.fori_loop(1, group, one, 0)
        inbound[kind, mine] = box[kind, mine]

    def swap_arrived(kind, way, box, inbound):
        def one(by, carry):
            swap_copy(kind, way, by, box, inbound).wait_recv()
            return carry

        lax.fori_loop(1, group, one, 0)

    def make_slots(kind):
        source = (tokens, out_grad)[kind]
        left = []
        for image in range(images):
            soft = soft_weights(logits_ref[image], 1 - kind)
            if kind == 1:
                combine[image] = soft
            row, slot = iota((packed, slots), 0), iota((packed, slots), 1)
            spread = zero_one((slot == (row // 8) * 2 + row % 2) & ((row // 2) % 2 == image))
            left.append(jnp.dot(spread, soft.astype(BF16), preferred_element_type=F32).astype(BF16))
        slot = jnp.dot(jnp.concatenate(left, axis=1), source[...].reshape(images * length, depth),
                       preferred_element_type=F32)
        first = (iota((packed, depth // 2), 0) // 4) % 2 == 0
        outbox[kind] = tiled(jnp.where(first, slot[:, :depth // 2], slot[:, depth // 2:]), group)

    def own_rows(kind):
        swap_arrived(kind, 0, outbox, inbox)
        block = unpack(inbox[kind], depth, True, own)
        rows[kind, z, x] = block[:count]
        other[kind, z] = block[count:]

    def send_back(kind):
        back_outbox[kind] = tiled(pack(total[kind].reshape(members * count, depth), own), group)
        swap_start(kind, 1, back_outbox, back_inbox)

    def finish(kind):
        swap_arrived(kind, 1, back_outbox, back_inbox)
        back = unpack(back_inbox[kind], depth, False)
        if kind == 1:
            slot_in_grad_ref[...] = back
            return
        for image in range(images):
            grad = lax.dot_general(back[image * slots:(image + 1) * slots], out_grad[image],
                                   (((1,), (1,)), ((), ())), preferred_element_type=F32)
            soft = combine[image]
            from_combine_ref[image] = soft * (grad - jnp.sum(soft * grad, axis=0, keepdims=True))

    sent = []
    flying = {}

    def send(key, source, target, there):
        copy = pltpu.make_async_remote_copy(
            src_ref=source, dst_ref=target,
            send_sem=send_sem.at[len(sent)], recv_sem=recv_sem.at[len(sent)],
            device_id={"dp": there}, device_id_type=MESH,
        )
        copy.start()
        sent.append(copy)
        flying[key] = copy

    def arrived(*key):
        flying.pop(key).wait_recv()

    tasks = {}

    def task(*name):
        def keep(run):
            tasks[name] = run
            return run

        return keep

    def gather(kind):
        def z_pieces(at):
            return rows.at[kind, at, x, :, first], other.at[kind, at, :, first]

        @task("g1", kind)
        def _():
            for way in range(2):
                for i, piece in enumerate(z_pieces(z)):
                    send(("g1", kind, way, i), piece, piece, z_dev[way])

        for way in range(2):
            @task("g2t", kind, way)
            def _(way=way):
                for i in range(2):
                    arrived("g1", kind, way, i)
                piece = z_pieces(z_from[way])[way]
                send(("g2", kind, way), piece, piece, z_dev[way])

        def along_x(name, at, features):
            here = rows.at[kind, at, x, :, features]
            send(name + ("twin",), here, here, twin_dev)
            send(name + ("mate",), other.at[kind, at, :, features], here, mate_dev)

        def from_mate(name, at, features):
            arrived(*name, "mate")
            piece = rows.at[kind, at, mate, :, features]
            send(name + ("beyond",), piece, piece, twin_dev)

        for c in range(RING):
            @task("s1", kind, c)
            def _(c=c):
                if c == 3:
                    for way in range(2):
                        arrived("g2", kind, way)
                along_x(("s1", kind, c), chunk[c], first)

            @task("s2t", kind, c)
            def _(c=c):
                from_mate(("s1", kind, c), chunk[c], first)

            @task("g", kind, c)
            def _(c=c):
                arrived("s1", kind, c, "twin")
                arrived("s1", kind, c, "beyond")

        @task("b1", kind)
        def _():
            along_x(("b1", kind), z, second)

        @task("b2t", kind)
        def _():
            from_mate(("b1", kind), z, second)

        for c in range(RING):
            @task("z1", kind, c)
            def _(c=c):
                if c >= 2:
                    arrived("b1", kind, ("twin", "beyond")[c - 2])
                piece = rows.at[kind, z, places[c], :, second]
                for way in range(2):
                    send(("z1", kind, c, way), piece, piece, z_dev[way])

            for way in range(2):
                @task("z2t", kind, c, way)
                def _(c=c, way=way):
                    arrived("z1", kind, c, way)
                    piece = rows.at[kind, z_from[way], places[c], halves[way], second]
                    send(("z2", kind, c, way), piece, piece, z_dev[way])

            @task("zg", kind, c)
            def _(c=c):
                for way in range(2):
                    arrived("z2", kind, c, way)

    def plus(*refs):
        value = refs[0][...].astype(F32)
        for ref in refs[1:]:
            value = value + ref[...].astype(F32)
        return value.astype(BF16)

    def reduce(kind):
        def to_twin(name, at, features, boxes):
            for i, place in enumerate((beyond, twin)):
                send(name + (i,), part.at[kind, at, place, :, features], boxes.at[i], twin_dev)

        def to_mate(name, at, features, boxes):
            arrived(*name, 0)
            piece = part.at[kind, at, mate, :, features]
            piece[...] = plus(piece, boxes.at[0])
            send(name + ("mate",), piece, other_part.at[kind, at, :, features], mate_dev)

        for c in range(RING):
            @task("r1", kind, c)
            def _(c=c):
                to_twin(("r1", kind, c), chunk[c], first, from_twin.at[kind, c])

            @task("r2t", kind, c)
            def _(c=c):
                to_mate(("r1", kind, c), chunk[c], first, from_twin.at[kind, c])

            @task("r", kind, c)
            def _(c=c):
                arrived("r1", kind, c, 1)
                arrived("r1", kind, c, "mate")
                piece = part.at[kind, chunk[c], x, :, first]
                piece[...] = plus(piece, from_twin.at[kind, c, 1])

        def z_pieces(at):
            return part.at[kind, at, x, :, first], other_part.at[kind, at, :, first]

        @task("t1", kind)
        def _():
            for way, piece in enumerate(z_pieces(chunk[3])):
                send(("t1", kind, way), piece, last_half.at[kind, way], z_dev[way])

        for way in range(2):
            @task("t2t", kind, way)
            def _(way=way):
                arrived("t1", kind, way)
                pieces = z_pieces(z_to[way])
                pieces[way][...] = plus(pieces[way], last_half.at[kind, way])
                for i, piece in enumerate(pieces):
                    send(("t2", kind, way, i), piece, last_full.at[kind, way, i], z_dev[way])

        @task("t", kind)
        def _():
            for i, piece in enumerate(z_pieces(z)):
                for way in range(2):
                    arrived("t2", kind, way, i)
                total[kind, i, :, first] = plus(piece, last_full.at[kind, 0, i], last_full.at[kind, 1, i])

        for c in range(RING):
            @task("q1", kind, c)
            def _(c=c):
                for way in range(2):
                    send(("q1", kind, c, way), part.at[kind, chunk[3], places[c], halves[way], second],
                         side_half.at[kind, c, way], z_dev[way])

            for way in range(2):
                @task("q2t", kind, c, way)
                def _(c=c, way=way):
                    arrived("q1", kind, c, way)
                    piece = part.at[kind, z_to[way], places[c], halves[way], second]
                    piece[...] = plus(piece, side_half.at[kind, c, way])
                    send(("q2", kind, c, way), part.at[kind, z_to[way], places[c], :, second],
                         side_full.at[kind, c, way], z_dev[way])

            @task("q", kind, c)
            def _(c=c):
                for way in range(2):
                    arrived("q2", kind, c, way)
                piece = part.at[kind, z, places[c], :, second]
                piece[...] = plus(piece, side_full.at[kind, c, 0], side_full.at[kind, c, 1])

        @task("v1", kind)
        def _():
            to_twin(("v1", kind), z, second, side_twin.at[kind])

        @task("v2t", kind)
        def _():
            to_mate(("v1", kind), z, second, side_twin.at[kind])

        @task("v", kind)
        def _():
            arrived("v1", kind, 1)
            arrived("v1", kind, "mate")
            total[kind, 0, :, second] = plus(part.at[kind, z, x, :, second], side_twin.at[kind, 1])
            total[kind, 1, :, second] = other_part[kind, z, :, second]

    def chunk_rows(kind, c):
        return rows[kind, chunk[c]].reshape(RING * count, depth)

    def place(c):
        return pl.ds(pl.multiple_of(chunk[c] * (RING * count), RING * count), RING * count)

    def forward(c):
        pre = lax.dot_general(chunk_rows(0, c), weights[0], (((1,), (1,)), ((), ())),
                              preferred_element_type=F32)
        cdf = normal_cdf(pre)
        act = (pre * cdf).astype(BF16)
        slope[place(c)] = cdf + pre * jnp.exp(-0.5 * pre * pre) * 0.3989422804014327
        hidden[place(c)] = act
        out = jnp.dot(act, weights[1], preferred_element_type=F32)
        part[0, chunk[c]] = out.astype(BF16).reshape(RING, count, depth)

    def backward(c):
        grad = lax.dot_general(chunk_rows(1, c), weights[1], (((1,), (1,)), ((), ())),
                               preferred_element_type=F32)
        grad = (grad * slope[place(c)]).astype(BF16)
        pre_grad[place(c)] = grad
        out = jnp.dot(grad, weights[0], preferred_element_type=F32)
        part[1, chunk[c]] = out.astype(BF16).reshape(RING, count, depth)

    def weight_grad(kind):
        left = (pre_grad, hidden)[kind][...]
        for part_at in range(2):
            columns = pl.ds(part_at * (depth // 2), depth // 2)
            right = rows[kind, :, :, :, columns].reshape(RING * RING * count, depth // 2)
            weight_grads[kind, :, columns] = lax.dot_general(
                left, right, (((0,), (0,)), ((), ())), preferred_element_type=F32).astype(BF16)

    piece_rows = width // PIECES

    def weight_piece(i):
        matrix, at = i // PIECES, i % PIECES * piece_rows
        send(("w", i), (w_in_ref, w_out_ref)[matrix].at[1 - own, pl.ds(at, piece_rows)],
             weights.at[matrix, pl.ds(width + at, piece_rows)], mate_dev)

    def grad_piece(kind, i):
        at = i * piece_rows
        send(("d", kind, i), weight_grads.at[kind, pl.ds(width + at, piece_rows)],
             mate_grads.at[kind, pl.ds(at, piece_rows)], mate_dev)

    outs = (w_in_grad_ref, w_out_grad_ref)
    stores = []

    def store(kind):
        for i in range(PIECES):
            arrived("d", kind, i)
        for i, source in enumerate((weight_grads.at[kind, pl.ds(0, width)], mate_grads.at[kind])):
            stores.append(pltpu.make_async_copy(
                source, outs[kind].at[(own, 1 - own)[i]], store_sem.at[kind, i]))
            stores[-1].start()

    @task("enter")
    def _():
        make_slots(0)
        pl.semaphore_wait(barrier, 4 + group - 1)

    @task("weights")
    def _():
        for i in range(2 * PIECES):
            arrived("w", i)
        for load in loads:
            load.wait()

    for i in range(2 * PIECES):
        tasks["ws", i] = lambda i=i: weight_piece(i)
    for kind in range(2):
        @task("make", kind)
        def _(kind=kind):
            if kind == 1:
                make_slots(1)
            swap_start(kind, 0, outbox, inbox)

        tasks["own", kind] = lambda kind=kind: own_rows(kind)
        gather(kind)
        reduce(kind)
        for c in range(RING):
            tasks["part", kind, c] = lambda kind=kind, c=c: (forward, backward)[kind](c)
        tasks["back", kind] = lambda kind=kind: send_back(kind)
        tasks["finish", kind] = lambda kind=kind: finish(kind)
        tasks["weight", kind] = lambda kind=kind: weight_grad(kind)
        for i in range(PIECES):
            tasks["ds", kind, i] = lambda kind=kind, i=i: grad_piece(kind, i)
        tasks["store", kind] = lambda kind=kind: store(kind)

    assert sorted(tasks, key=str) == sorted(ORDER, key=str)
    for name in ORDER:
        tasks[name]()
    assert not flying and len(sent) == COPIES

    for copy in sent:
        copy.wait_send()

    def swapped(by, carry):
        for kind in range(2):
            swap_copy(kind, 0, by, outbox, inbox).wait_send()
            swap_copy(kind, 1, by, back_outbox, back_inbox).wait_send()
        return carry

    lax.fori_loop(1, group, swapped, 0)
    for copy in stores:
        copy.wait()


def last_kernel(
    tokens, logits_ref, slot_in_grad_ref, from_combine_ref, w_in_grad_ref, w_out_grad_ref,
    token_grad_ref, logit_grad_ref, w_in_out_ref, w_out_out_ref,
    token_grad, sem, token_sem,
):
    images, slots, _ = logits_ref.shape
    moves = [
        pltpu.make_async_copy(source.at[e], target.at[e], sem.at[2 * i + e])
        for i, (source, target) in enumerate(
            ((w_in_grad_ref, w_in_out_ref), (w_out_grad_ref, w_out_out_ref)))
        for e in range(2)
    ]
    for move in moves:
        move.start()
    softs = []
    for image in range(images):
        back = slot_in_grad_ref[image * slots:(image + 1) * slots]
        softs.append(soft_weights(logits_ref[image], 1))
        token_grad[image] = lax.dot_general(
            softs[image].astype(BF16), back, (((0,), (0,)), ((), ())), preferred_element_type=F32
        ).astype(BF16)
        moves.append(pltpu.make_async_copy(token_grad.at[image], token_grad_ref.at[image], token_sem.at[image]))
        moves[-1].start()
    for image in range(images):
        back = slot_in_grad_ref[image * slots:(image + 1) * slots]
        grad = lax.dot_general(back, tokens[image], (((1,), (1,)), ((), ())), preferred_element_type=F32)
        soft = softs[image]
        grad = soft * (grad - jnp.sum(soft * grad, axis=1, keepdims=True))
        logit_grad_ref[image] = from_combine_ref[image] + grad
    for move in moves:
        move.wait()


def shards(tokens, logits, out_grad, w_in, w_out):
    images, length, depth = tokens.shape
    slots = logits.shape[2]
    logits = jnp.transpose(logits, (0, 2, 1))
    members, width, _ = w_in.shape
    group = slots // members
    count = group * images
    kept = (RING * RING * count, 2 * width)
    columns = depth // 2 // TILE
    swapped = (2, group, (columns + columns % 2) * 8, TILE)
    rest = depth - SPLIT
    shape = jax.ShapeDtypeStruct
    whole = pl.BlockSpec(memory_space=pl.ANY)
    inside = pl.BlockSpec(memory_space=pltpu.VMEM)
    far = pl.BlockSpec(memory_space=pltpu.HBM)
    slot_in_grad, from_combine, w_in_grad, w_out_grad = pl.pallas_call(
        kernel,
        out_shape=(
            shape((images * slots, depth), BF16),
            shape(logits.shape, F32),
            shape(w_in.shape, BF16),
            shape(w_out.shape, BF16),
        ),
        in_specs=[inside, inside, inside, far, far],
        out_specs=(inside, inside, whole, whole),
        scratch_shapes=[
            pltpu.VMEM(logits.shape, F32),
            pltpu.VMEM(swapped, BF16),
            pltpu.VMEM(swapped, BF16),
            pltpu.VMEM(swapped, BF16),
            pltpu.VMEM(swapped, BF16),
            pltpu.VMEM((2, RING, RING, count, depth), BF16),
            pltpu.VMEM((2, RING, count, depth), BF16),
            pltpu.VMEM((2, RING, RING, count, depth), BF16),
            pltpu.VMEM((2, RING, count, depth), BF16),
            pltpu.VMEM((2, RING, 2, count, SPLIT), BF16),
            pltpu.VMEM((2, 2, count, SPLIT), BF16),
            pltpu.VMEM((2, 2, 2, count, SPLIT), BF16),
            pltpu.VMEM((2, RING, 2, count // 2, rest), BF16),
            pltpu.VMEM((2, RING, 2, count, rest), BF16),
            pltpu.VMEM((2, 2, count, rest), BF16),
            pltpu.VMEM((2, 2, count, depth), BF16),
            pltpu.VMEM((2, 2 * width, depth), BF16),
            pltpu.VMEM((2, 2 * width, depth), BF16),
            pltpu.VMEM((2, width, depth), BF16),
            pltpu.VMEM(kept, F32),
            pltpu.VMEM(kept, BF16),
            pltpu.VMEM(kept, BF16),
            pltpu.SemaphoreType.DMA((2,)),
            pltpu.SemaphoreType.DMA((2, 2)),
            pltpu.SemaphoreType.DMA((2, 2, group)),
            pltpu.SemaphoreType.DMA((2, 2, group)),
            pltpu.SemaphoreType.DMA((COPIES,)),
            pltpu.SemaphoreType.DMA((COPIES,)),
        ],
        compiler_params=pltpu.CompilerParams(
            collective_id=0, has_side_effects=True, vmem_limit_bytes=48 * 2**20
        ),
    )(tokens, logits, out_grad, w_in, w_out)
    token_grad, logit_grad, w_in_grad, w_out_grad = pl.pallas_call(
        last_kernel,
        out_shape=(
            shape(tokens.shape, BF16),
            shape(logits.shape, F32),
            shape(w_in.shape, BF16),
            shape(w_out.shape, BF16),
        ),
        in_specs=[inside, inside, inside, inside, whole, whole],
        out_specs=(whole, inside, whole, whole),
        scratch_shapes=[
            pltpu.VMEM(tokens.shape, BF16),
            pltpu.SemaphoreType.DMA((4,)),
            pltpu.SemaphoreType.DMA((2,)),
        ],
        compiler_params=pltpu.CompilerParams(vmem_limit_bytes=16 * 2**20),
    )(tokens, logits, slot_in_grad, from_combine, w_in_grad, w_out_grad)
    return token_grad, jnp.transpose(logit_grad, (0, 2, 1)), w_in_grad, w_out_grad


def solution(mesh):
    placed = (
        P(("dp", "expert"), None, None),
        P(("dp", "expert"), None, None),
        P(("dp", "expert"), None, None),
        P("expert", "dp", None),
        P("expert", "dp", None),
    )
    return jax.shard_map(
        shards,
        mesh=mesh,
        in_specs=placed,
        out_specs=(
            P(("dp", "expert"), None, None),
            P(("dp", "expert"), None, None),
            P("expert", "dp", None),
            P("expert", "dp", None),
        ),
        check_vma=False,
    )
```

```python
import jax
import jax.numpy as jnp
from jax import lax
from jax.experimental import pallas as pl
from jax.experimental.pallas import tpu as pltpu
from jax.sharding import PartitionSpec as P

RING = 4
TILE = 128
SPLIT = 768
LAG = 90
PIECES = 5
COPIES = 2 * 74 + 4 * PIECES
MESH = pl.DeviceIdType.MESH
BF16 = jnp.bfloat16
F32 = jnp.float32


def normal_cdf(values):
    return 0.5 * (1.0 + lax.erf(values * 0.7071067811865476))


def soft_weights(values, over_dim):
    highest = jnp.max(values, axis=over_dim, keepdims=True)
    raised = jnp.exp(values - highest)
    return raised / jnp.sum(raised, axis=over_dim, keepdims=True)


def shift(at, by, size):
    return lax.rem(at + (by + size), size)


def iota(shape, dim):
    return lax.broadcasted_iota(jnp.int32, shape, dim)


def zero_one(mask):
    return mask.astype(F32).astype(BF16)


def tiled(block, group):
    packed, features = block.shape
    pieces = [
        block[:, at * TILE:(at + 1) * TILE].reshape(group, 1, packed // group, TILE)
        for at in range(features // TILE)
    ]
    if len(pieces) % 2:
        pieces.append(jnp.zeros_like(pieces[0]))
    block = jnp.concatenate(pieces, axis=1)
    return block.reshape(group, len(pieces) * (packed // group), TILE).astype(BF16)


def untiled(block, features):
    group, high, _ = block.shape
    block = block.astype(F32).reshape(group, high // 8, 8, TILE)
    return jnp.concatenate(
        [block[:, at].reshape(group * 8, TILE) for at in range(features // TILE)], axis=1
    ).astype(BF16)


def picker(packed, half, by_member, lead):
    shape = (packed // 2, packed)
    row, column = iota(shape, 0), iota(shape, 1)
    first, source, second = row // (packed // 4), (row % (packed // 4)) // 2, row % 2
    image, member = (second, (first + lead) % 2) if by_member else (first, second)
    return zero_one(column == ((source * 2 + half) * 2 + image) * 2 + member)


def unpack(block, depth, by_member, lead=0):
    block = untiled(block, depth // 2)
    return jnp.concatenate(
        [jnp.dot(picker(block.shape[0], half, by_member, lead), block, preferred_element_type=F32)
         for half in range(2)],
        axis=1,
    ).astype(BF16)


def pack(block, lead):
    rows, depth = block.shape
    return sum(
        lax.dot_general(picker(2 * rows, half, True, lead), block[:, half * depth // 2:(half + 1) * depth // 2],
                        (((0,), (0,)), ((), ())), preferred_element_type=F32)
        for half in range(2)
    )


ORDER = (
    ("enter",), ("ws", 6), ("make", 0), ("ws", 7), ("make", 1), ("ws", 5), ("ws", 4), ("own", 0), ("z1", 0, 0),
    ("b1", 0), ("g1", 0), ("s1", 0, 0), ("ws", 9), ("b2t", 0), ("ws", 0), ("ws", 2), ("own", 1), ("z1", 0, 1),
    ("ws", 8), ("z1", 0, 2), ("z1", 0, 3), ("g2t", 0, 0), ("z2t", 0, 0, 1), ("g2t", 0, 1), ("s1", 0, 1),
    ("z2t", 0, 1, 0), ("s1", 0, 2), ("s2t", 0, 0), ("z2t", 0, 1, 1), ("z2t", 0, 0, 0), ("b1", 1), ("ws", 3),
    ("z2t", 0, 2, 1), ("z2t", 0, 2, 0), ("z2t", 0, 3, 0), ("z2t", 0, 3, 1), ("ws", 1), ("g1", 1), ("s2t", 0, 1),
    ("z1", 1, 0), ("s1", 0, 3), ("b2t", 1), ("zg", 0, 2), ("zg", 0, 3), ("zg", 0, 0), ("g", 0, 0), ("s1", 1, 0),
    ("zg", 0, 1), ("z1", 1, 2), ("s2t", 0, 2), ("z1", 1, 1), ("weights",), ("part", 0, 0), ("s2t", 0, 3),
    ("r1", 0, 0), ("z1", 1, 3), ("g2t", 1, 1), ("s1", 1, 2), ("g", 0, 1), ("g2t", 1, 0), ("part", 0, 1),
    ("s1", 1, 1), ("r1", 0, 1), ("s2t", 1, 0), ("z2t", 1, 0, 1), ("g", 0, 3), ("part", 0, 3), ("r1", 0, 3),
    ("z2t", 1, 0, 0), ("z2t", 1, 2, 1), ("g", 0, 2), ("z2t", 1, 2, 0), ("z2t", 1, 1, 0), ("z2t", 1, 1, 1),
    ("part", 0, 2), ("q1", 0, 2), ("z2t", 1, 3, 1), ("s2t", 1, 2), ("z2t", 1, 3, 0), ("q1", 0, 1), ("q1", 0, 3),
    ("r2t", 0, 3), ("q1", 0, 0), ("s1", 1, 3), ("s2t", 1, 1), ("zg", 1, 0), ("r1", 0, 2), ("q2t", 0, 2, 0),
    ("r2t", 0, 1), ("r2t", 0, 0), ("zg", 1, 2), ("g", 1, 0), ("g", 1, 2), ("q2t", 0, 2, 1), ("zg", 1, 1),
    ("r", 0, 3), ("t1", 0), ("zg", 1, 3), ("part", 1, 0), ("s2t", 1, 3), ("r1", 1, 0), ("q2t", 0, 0, 1),
    ("q2t", 0, 3, 0), ("q2t", 0, 3, 1), ("part", 1, 2), ("r2t", 0, 2), ("q2t", 0, 1, 1), ("r1", 1, 2),
    ("g", 1, 1), ("q2t", 0, 1, 0), ("part", 1, 1), ("r1", 1, 1), ("g", 1, 3), ("q2t", 0, 0, 0), ("part", 1, 3),
    ("q1", 1, 2), ("r", 0, 2), ("q", 0, 2), ("q1", 1, 0), ("q1", 1, 1), ("r", 0, 1), ("q1", 1, 3), ("r1", 1, 3),
    ("r2t", 1, 0), ("weight", 1), ("ds", 1, 4), ("t2t", 0, 1), ("t2t", 0, 0), ("q", 0, 3), ("r2t", 1, 2),
    ("weight", 0), ("r2t", 1, 3), ("v1", 0), ("q2t", 1, 3, 0), ("q", 0, 0), ("ds", 0, 1), ("r", 0, 0),
    ("q2t", 1, 3, 1), ("r", 1, 3), ("r2t", 1, 1), ("ds", 1, 3), ("t1", 1), ("q2t", 1, 2, 1), ("q", 0, 1),
    ("q2t", 1, 2, 0), ("r", 1, 2), ("r", 1, 0), ("q2t", 1, 1, 0), ("q2t", 1, 1, 1), ("v2t", 0),
    ("q2t", 1, 0, 0), ("ds", 0, 4), ("ds", 1, 1), ("q2t", 1, 0, 1), ("q", 1, 3), ("r", 1, 1), ("ds", 0, 2),
    ("v", 0), ("t", 0), ("back", 0), ("q", 1, 2), ("t2t", 1, 1), ("t2t", 1, 0), ("v1", 1), ("ds", 1, 2),
    ("q", 1, 1), ("v2t", 1), ("ds", 0, 0), ("ds", 1, 0), ("q", 1, 0), ("finish", 0), ("ds", 0, 3), ("v", 1),
    ("t", 1), ("back", 1), ("store", 0), ("store", 1), ("finish", 1),
)


def kernel(
    tokens, logits_ref, out_grad, w_in_ref, w_out_ref,
    slot_in_grad_ref, from_combine_ref, w_in_grad_ref, w_out_grad_ref,
    combine, outbox, inbox, back_outbox, back_inbox,
    rows, other, part, other_part, from_twin, last_half, last_full, side_half, side_full, side_twin, total,
    weights, weight_grads, mate_grads, slope, hidden, pre_grad,
    load_sem, store_sem, swap_send, swap_recv, send_sem, recv_sem,
):
    count, depth = rows.shape[3:]
    width = weights.shape[1] // 2
    images, slots, length = combine.shape
    members = 2
    group = slots // members
    packed = group * 2 * images * members
    me = lax.axis_index("dp")
    mine = lax.axis_index("expert")
    z, x = me // RING, lax.rem(me, RING)
    z_to = (shift(z, 1, RING), shift(z, -1, RING))
    z_from = (z_to[1], z_to[0])
    chunk = (z, z_from[0], z_from[1], shift(z, 2, RING))
    z_dev = tuple(to * RING + x for to in z_to)
    turn = lax.rem(mine, 2)
    turned = shift(x, turn, RING)
    mate = shift(turned + 1 - 2 * lax.rem(turned, 2), RING - turn, RING)
    twin = shift(RING - 1 - turned, RING - turn, RING)
    beyond = shift(x, 2, RING)
    places = (x, mate, twin, beyond)
    mate_dev, twin_dev = z * RING + mate, z * RING + twin
    own = lax.rem((turned + 1) // 2, 2)
    first, second = pl.ds(0, SPLIT), pl.ds(SPLIT, depth - SPLIT)
    halves = (pl.ds(0, count // 2), pl.ds(count // 2, count // 2))

    def partner(by):
        return lax.rem(mine + by, group)

    barrier = pltpu.get_barrier_semaphore()
    for there in z_dev + (mate_dev, twin_dev):
        pl.semaphore_signal(barrier, inc=1, device_id={"dp": there}, device_id_type=MESH)

    def greet(by, carry):
        pl.semaphore_signal(barrier, inc=1, device_id={"expert": partner(by)}, device_id_type=MESH)
        return carry

    lax.fori_loop(1, group, greet, 0)

    loads = [
        pltpu.make_async_copy(source.at[own], weights.at[i, pl.ds(0, width)], load_sem.at[i])
        for i, source in enumerate((w_in_ref, w_out_ref))
    ]
    for load in loads:
        load.start()

    def swap_copy(kind, way, by, box, inbound):
        return pltpu.make_async_remote_copy(
            src_ref=box.at[kind, partner(by)], dst_ref=inbound.at[kind, mine],
            send_sem=swap_send.at[way, kind, by], recv_sem=swap_recv.at[way, kind, by],
            device_id={"expert": partner(by)}, device_id_type=MESH,
        )

    def swap_start(kind, way, box, inbound):
        for by in range(1, group):
            swap_copy(kind, way, by, box, inbound).start()
        inbound[kind, mine] = box[kind, mine]

    def swap_arrived(kind, way, box, inbound):
        for by in range(1, group):
            swap_copy(kind, way, by, box, inbound).wait_recv()

    def swap_sent(kind, way, box, inbound):
        for by in range(1, group):
            swap_copy(kind, way, by, box, inbound).wait_send()

    def make_slots(kind):
        source = (tokens, out_grad)[kind]
        left = []
        for image in range(images):
            soft = soft_weights(logits_ref[image], 1 - kind)
            if kind == 1:
                combine[image] = soft
            row, slot = iota((packed, slots), 0), iota((packed, slots), 1)
            spread = zero_one((slot == (row // 8) * 2 + row % 2) & ((row // 2) % 2 == image))
            left.append(jnp.dot(spread, soft.astype(BF16), preferred_element_type=F32).astype(BF16))
        slot = jnp.dot(jnp.concatenate(left, axis=1), source[...].reshape(images * length, depth),
                       preferred_element_type=F32)
        first = (iota((packed, depth // 2), 0) // 4) % 2 == 0
        outbox[kind] = tiled(jnp.where(first, slot[:, :depth // 2], slot[:, depth // 2:]), group)

    def own_rows(kind):
        swap_arrived(kind, 0, outbox, inbox)
        block = unpack(inbox[kind], depth, True, own)
        rows[kind, z, x] = block[:count]
        other[kind, z] = block[count:]

    def send_back(kind):
        back_outbox[kind] = tiled(pack(total[kind].reshape(members * count, depth), own), group)
        swap_start(kind, 1, back_outbox, back_inbox)

    def finish(kind):
        swap_arrived(kind, 1, back_outbox, back_inbox)
        back = unpack(back_inbox[kind], depth, False)
        if kind == 1:
            slot_in_grad_ref[...] = back
            return
        swap_sent(0, 1, back_outbox, back_inbox)
        for image in range(images):
            grad = lax.dot_general(back[image * slots:(image + 1) * slots], out_grad[image],
                                   (((1,), (1,)), ((), ())), preferred_element_type=F32)
            soft = combine[image]
            from_combine_ref[image] = soft * (grad - jnp.sum(soft * grad, axis=0, keepdims=True))

    sent = []
    flying = {}

    def send(key, source, target, there):
        copy = pltpu.make_async_remote_copy(
            src_ref=source, dst_ref=target,
            send_sem=send_sem.at[len(sent)], recv_sem=recv_sem.at[len(sent)],
            device_id={"dp": there}, device_id_type=MESH,
        )
        copy.start()
        sent.append(copy)
        flying[key] = copy

    def arrived(*key):
        flying.pop(key).wait_recv()

    tasks = {}

    def task(*name):
        def keep(run):
            tasks[name] = run
            return run

        return keep

    def gather(kind):
        def z_pieces(at):
            return rows.at[kind, at, x, :, first], other.at[kind, at, :, first]

        @task("g1", kind)
        def _():
            for way in range(2):
                for i, piece in enumerate(z_pieces(z)):
                    send(("g1", kind, way, i), piece, piece, z_dev[way])

        for way in range(2):
            @task("g2t", kind, way)
            def _(way=way):
                for i in range(2):
                    arrived("g1", kind, way, i)
                piece = z_pieces(z_from[way])[way]
                send(("g2", kind, way), piece, piece, z_dev[way])

        def along_x(name, at, features):
            here = rows.at[kind, at, x, :, features]
            send(name + ("twin",), here, here, twin_dev)
            send(name + ("mate",), other.at[kind, at, :, features], here, mate_dev)

        def from_mate(name, at, features):
            arrived(*name, "mate")
            piece = rows.at[kind, at, mate, :, features]
            send(name + ("beyond",), piece, piece, twin_dev)

        for c in range(RING):
            @task("s1", kind, c)
            def _(c=c):
                if c == 3:
                    for way in range(2):
                        arrived("g2", kind, way)
                along_x(("s1", kind, c), chunk[c], first)

            @task("s2t", kind, c)
            def _(c=c):
                from_mate(("s1", kind, c), chunk[c], first)

            @task("g", kind, c)
            def _(c=c):
                arrived("s1", kind, c, "twin")
                arrived("s1", kind, c, "beyond")

        @task("b1", kind)
        def _():
            along_x(("b1", kind), z, second)

        @task("b2t", kind)
        def _():
            from_mate(("b1", kind), z, second)

        for c in range(RING):
            @task("z1", kind, c)
            def _(c=c):
                if c >= 2:
                    arrived("b1", kind, ("twin", "beyond")[c - 2])
                piece = rows.at[kind, z, places[c], :, second]
                for way in range(2):
                    send(("z1", kind, c, way), piece, piece, z_dev[way])

            for way in range(2):
                @task("z2t", kind, c, way)
                def _(c=c, way=way):
                    arrived("z1", kind, c, way)
                    piece = rows.at[kind, z_from[way], places[c], halves[way], second]
                    send(("z2", kind, c, way), piece, piece, z_dev[way])

            @task("zg", kind, c)
            def _(c=c):
                for way in range(2):
                    arrived("z2", kind, c, way)

    def plus(*refs):
        value = refs[0][...].astype(F32)
        for ref in refs[1:]:
            value = value + ref[...].astype(F32)
        return value.astype(BF16)

    def reduce(kind):
        def to_twin(name, at, features, boxes):
            for i, place in enumerate((beyond, twin)):
                send(name + (i,), part.at[kind, at, place, :, features], boxes.at[i], twin_dev)

        def to_mate(name, at, features, boxes):
            arrived(*name, 0)
            piece = part.at[kind, at, mate, :, features]
            piece[...] = plus(piece, boxes.at[0])
            send(name + ("mate",), piece, other_part.at[kind, at, :, features], mate_dev)

        for c in range(RING):
            @task("r1", kind, c)
            def _(c=c):
                to_twin(("r1", kind, c), chunk[c], first, from_twin.at[kind, c])

            @task("r2t", kind, c)
            def _(c=c):
                to_mate(("r1", kind, c), chunk[c], first, from_twin.at[kind, c])

            @task("r", kind, c)
            def _(c=c):
                arrived("r1", kind, c, 1)
                arrived("r1", kind, c, "mate")
                piece = part.at[kind, chunk[c], x, :, first]
                piece[...] = plus(piece, from_twin.at[kind, c, 1])

        def z_pieces(at):
            return part.at[kind, at, x, :, first], other_part.at[kind, at, :, first]

        @task("t1", kind)
        def _():
            for way, piece in enumerate(z_pieces(chunk[3])):
                send(("t1", kind, way), piece, last_half.at[kind, way], z_dev[way])

        for way in range(2):
            @task("t2t", kind, way)
            def _(way=way):
                arrived("t1", kind, way)
                pieces = z_pieces(z_to[way])
                pieces[way][...] = plus(pieces[way], last_half.at[kind, way])
                for i, piece in enumerate(pieces):
                    send(("t2", kind, way, i), piece, last_full.at[kind, way, i], z_dev[way])

        @task("t", kind)
        def _():
            for i, piece in enumerate(z_pieces(z)):
                for way in range(2):
                    arrived("t2", kind, way, i)
                total[kind, i, :, first] = plus(piece, last_full.at[kind, 0, i], last_full.at[kind, 1, i])

        for c in range(RING):
            @task("q1", kind, c)
            def _(c=c):
                for way in range(2):
                    send(("q1", kind, c, way), part.at[kind, chunk[3], places[c], halves[way], second],
                         side_half.at[kind, c, way], z_dev[way])

            for way in range(2):
                @task("q2t", kind, c, way)
                def _(c=c, way=way):
                    arrived("q1", kind, c, way)
                    piece = part.at[kind, z_to[way], places[c], halves[way], second]
                    piece[...] = plus(piece, side_half.at[kind, c, way])
                    send(("q2", kind, c, way), part.at[kind, z_to[way], places[c], :, second],
                         side_full.at[kind, c, way], z_dev[way])

            @task("q", kind, c)
            def _(c=c):
                for way in range(2):
                    arrived("q2", kind, c, way)
                piece = part.at[kind, z, places[c], :, second]
                piece[...] = plus(piece, side_full.at[kind, c, 0], side_full.at[kind, c, 1])

        @task("v1", kind)
        def _():
            to_twin(("v1", kind), z, second, side_twin.at[kind])

        @task("v2t", kind)
        def _():
            to_mate(("v1", kind), z, second, side_twin.at[kind])

        @task("v", kind)
        def _():
            arrived("v1", kind, 1)
            arrived("v1", kind, "mate")
            total[kind, 0, :, second] = plus(part.at[kind, z, x, :, second], side_twin.at[kind, 1])
            total[kind, 1, :, second] = other_part[kind, z, :, second]

    def chunk_rows(kind, c):
        return rows[kind, chunk[c]].reshape(RING * count, depth)

    def place(c):
        return pl.ds(pl.multiple_of(chunk[c] * (RING * count), RING * count), RING * count)

    def forward(c):
        pre = lax.dot_general(chunk_rows(0, c), weights[0], (((1,), (1,)), ((), ())),
                              preferred_element_type=F32)
        cdf = normal_cdf(pre)
        act = (pre * cdf).astype(BF16)
        slope[place(c)] = cdf + pre * jnp.exp(-0.5 * pre * pre) * 0.3989422804014327
        hidden[place(c)] = act
        out = jnp.dot(act, weights[1], preferred_element_type=F32)
        part[0, chunk[c]] = out.astype(BF16).reshape(RING, count, depth)

    def backward(c):
        grad = lax.dot_general(chunk_rows(1, c), weights[1], (((1,), (1,)), ((), ())),
                               preferred_element_type=F32)
        grad = (grad * slope[place(c)]).astype(BF16)
        pre_grad[place(c)] = grad
        out = jnp.dot(grad, weights[0], preferred_element_type=F32)
        part[1, chunk[c]] = out.astype(BF16).reshape(RING, count, depth)

    def weight_grad(kind):
        left = (pre_grad, hidden)[kind][...]
        for part_at in range(2):
            columns = pl.ds(part_at * (depth // 2), depth // 2)
            right = rows[kind, :, :, :, columns].reshape(RING * RING * count, depth // 2)
            weight_grads[kind, :, columns] = lax.dot_general(
                left, right, (((0,), (0,)), ((), ())), preferred_element_type=F32).astype(BF16)

    piece_rows = width // PIECES

    def weight_piece(i):
        matrix, at = i // PIECES, i % PIECES * piece_rows
        send(("w", i), (w_in_ref, w_out_ref)[matrix].at[1 - own, pl.ds(at, piece_rows)],
             weights.at[matrix, pl.ds(width + at, piece_rows)], mate_dev)

    def grad_piece(kind, i):
        at = i * piece_rows
        send(("d", kind, i), weight_grads.at[kind, pl.ds(width + at, piece_rows)],
             mate_grads.at[kind, pl.ds(at, piece_rows)], mate_dev)

    outs = (w_in_grad_ref, w_out_grad_ref)
    stores = []

    def store(kind):
        for i in range(PIECES):
            arrived("d", kind, i)
        for i, source in enumerate((weight_grads.at[kind, pl.ds(0, width)], mate_grads.at[kind])):
            stores.append(pltpu.make_async_copy(
                source, outs[kind].at[(own, 1 - own)[i]], store_sem.at[kind, i]))
            stores[-1].start()

    @task("enter")
    def _():
        make_slots(0)
        pl.semaphore_wait(barrier, 4 + group - 1)

    @task("weights")
    def _():
        for i in range(2 * PIECES):
            arrived("w", i)
        for load in loads:
            load.wait()
        for kind in range(2):
            swap_sent(kind, 0, outbox, inbox)

    for i in range(2 * PIECES):
        tasks["ws", i] = lambda i=i: weight_piece(i)
    for kind in range(2):
        @task("make", kind)
        def _(kind=kind):
            if kind == 1:
                make_slots(1)
            swap_start(kind, 0, outbox, inbox)

        tasks["own", kind] = lambda kind=kind: own_rows(kind)
        gather(kind)
        reduce(kind)
        for c in range(RING):
            tasks["part", kind, c] = lambda kind=kind, c=c: (forward, backward)[kind](c)
        tasks["back", kind] = lambda kind=kind: send_back(kind)
        tasks["finish", kind] = lambda kind=kind: finish(kind)
        tasks["weight", kind] = lambda kind=kind: weight_grad(kind)
        for i in range(PIECES):
            tasks["ds", kind, i] = lambda kind=kind, i=i: grad_piece(kind, i)
        tasks["store", kind] = lambda kind=kind: store(kind)

    assert sorted(tasks, key=str) == sorted(ORDER, key=str)
    counts, waited = [], 0
    for at, name in enumerate(ORDER):
        tasks[name]()
        counts.append(len(sent))
        while at >= LAG and waited < counts[at - LAG]:
            sent[waited].wait_send()
            waited += 1
    assert not flying and len(sent) == COPIES
    for copy in sent[waited:]:
        copy.wait_send()
    swap_sent(1, 1, back_outbox, back_inbox)
    for copy in stores:
        copy.wait()


def last_kernel(
    tokens, logits_ref, slot_in_grad_ref, from_combine_ref, w_in_grad_ref, w_out_grad_ref,
    token_grad_ref, logit_grad_ref, w_in_out_ref, w_out_out_ref,
    token_grad, sem, token_sem,
):
    images, slots, _ = logits_ref.shape
    moves = [
        pltpu.make_async_copy(source.at[e], target.at[e], sem.at[2 * i + e])
        for i, (source, target) in enumerate(
            ((w_in_grad_ref, w_in_out_ref), (w_out_grad_ref, w_out_out_ref)))
        for e in range(2)
    ]
    for move in moves:
        move.start()
    softs = []
    for image in range(images):
        back = slot_in_grad_ref[image * slots:(image + 1) * slots]
        softs.append(soft_weights(logits_ref[image], 1))
        token_grad[image] = lax.dot_general(
            softs[image].astype(BF16), back, (((0,), (0,)), ((), ())), preferred_element_type=F32
        ).astype(BF16)
        moves.append(pltpu.make_async_copy(token_grad.at[image], token_grad_ref.at[image], token_sem.at[image]))
        moves[-1].start()
    for image in range(images):
        back = slot_in_grad_ref[image * slots:(image + 1) * slots]
        grad = lax.dot_general(back, tokens[image], (((1,), (1,)), ((), ())), preferred_element_type=F32)
        soft = softs[image]
        grad = soft * (grad - jnp.sum(soft * grad, axis=1, keepdims=True))
        logit_grad_ref[image] = from_combine_ref[image] + grad
    for move in moves:
        move.wait()


def shards(tokens, logits, out_grad, w_in, w_out):
    images, length, depth = tokens.shape
    slots = logits.shape[2]
    logits = jnp.transpose(logits, (0, 2, 1))
    members, width, _ = w_in.shape
    group = slots // members
    count = group * images
    kept = (RING * RING * count, 2 * width)
    columns = depth // 2 // TILE
    swapped = (2, group, (columns + columns % 2) * 8, TILE)
    rest = depth - SPLIT
    shape = jax.ShapeDtypeStruct
    whole = pl.BlockSpec(memory_space=pl.ANY)
    inside = pl.BlockSpec(memory_space=pltpu.VMEM)
    far = pl.BlockSpec(memory_space=pltpu.HBM)
    slot_in_grad, from_combine, w_in_grad, w_out_grad = pl.pallas_call(
        kernel,
        out_shape=(
            shape((images * slots, depth), BF16),
            shape(logits.shape, F32),
            shape(w_in.shape, BF16),
            shape(w_out.shape, BF16),
        ),
        in_specs=[inside, inside, inside, far, far],
        out_specs=(inside, inside, whole, whole),
        scratch_shapes=[
            pltpu.VMEM(logits.shape, F32),
            pltpu.VMEM(swapped, BF16),
            pltpu.VMEM(swapped, BF16),
            pltpu.VMEM(swapped, BF16),
            pltpu.VMEM(swapped, BF16),
            pltpu.VMEM((2, RING, RING, count, depth), BF16),
            pltpu.VMEM((2, RING, count, depth), BF16),
            pltpu.VMEM((2, RING, RING, count, depth), BF16),
            pltpu.VMEM((2, RING, count, depth), BF16),
            pltpu.VMEM((2, RING, 2, count, SPLIT), BF16),
            pltpu.VMEM((2, 2, count, SPLIT), BF16),
            pltpu.VMEM((2, 2, 2, count, SPLIT), BF16),
            pltpu.VMEM((2, RING, 2, count // 2, rest), BF16),
            pltpu.VMEM((2, RING, 2, count, rest), BF16),
            pltpu.VMEM((2, 2, count, rest), BF16),
            pltpu.VMEM((2, 2, count, depth), BF16),
            pltpu.VMEM((2, 2 * width, depth), BF16),
            pltpu.VMEM((2, 2 * width, depth), BF16),
            pltpu.VMEM((2, width, depth), BF16),
            pltpu.VMEM(kept, F32),
            pltpu.VMEM(kept, BF16),
            pltpu.VMEM(kept, BF16),
            pltpu.SemaphoreType.DMA((2,)),
            pltpu.SemaphoreType.DMA((2, 2)),
            pltpu.SemaphoreType.DMA((2, 2, group)),
            pltpu.SemaphoreType.DMA((2, 2, group)),
            pltpu.SemaphoreType.DMA((COPIES,)),
            pltpu.SemaphoreType.DMA((COPIES,)),
        ],
        compiler_params=pltpu.CompilerParams(
            collective_id=0, has_side_effects=True, vmem_limit_bytes=48 * 2**20
        ),
    )(tokens, logits, out_grad, w_in, w_out)
    token_grad, logit_grad, w_in_grad, w_out_grad = pl.pallas_call(
        last_kernel,
        out_shape=(
            shape(tokens.shape, BF16),
            shape(logits.shape, F32),
            shape(w_in.shape, BF16),
            shape(w_out.shape, BF16),
        ),
        in_specs=[inside, inside, inside, inside, whole, whole],
        out_specs=(whole, inside, whole, whole),
        scratch_shapes=[
            pltpu.VMEM(tokens.shape, BF16),
            pltpu.SemaphoreType.DMA((4,)),
            pltpu.SemaphoreType.DMA((2,)),
        ],
        compiler_params=pltpu.CompilerParams(vmem_limit_bytes=16 * 2**20),
    )(tokens, logits, slot_in_grad, from_combine, w_in_grad, w_out_grad)
    return token_grad, jnp.transpose(logit_grad, (0, 2, 1)), w_in_grad, w_out_grad


def solution(mesh):
    placed = (
        P(("dp", "expert"), None, None),
        P(("dp", "expert"), None, None),
        P(("dp", "expert"), None, None),
        P("expert", "dp", None),
        P("expert", "dp", None),
    )
    return jax.shard_map(
        shards,
        mesh=mesh,
        in_specs=placed,
        out_specs=(
            P(("dp", "expert"), None, None),
            P(("dp", "expert"), None, None),
            P("expert", "dp", None),
            P("expert", "dp", None),
        ),
        check_vma=False,
    )
```

```python
import jax
import jax.numpy as jnp
from jax import lax
from jax.experimental import pallas as pl
from jax.experimental.pallas import tpu as pltpu
from jax.sharding import PartitionSpec as P

RING = 4
TILE = 128
SPLIT = 768
LAG = 90
STORE_AT = {("v", 0): 25, ("finish", 0): 14}
PIECES = 5
COPIES = 2 * 74 + 4 * PIECES
MESH = pl.DeviceIdType.MESH
BF16 = jnp.bfloat16
F32 = jnp.float32


def normal_cdf(values):
    return 0.5 * (1.0 + lax.erf(values * 0.7071067811865476))


def soft_weights(values, over_dim):
    highest = jnp.max(values, axis=over_dim, keepdims=True)
    raised = jnp.exp(values - highest)
    return raised / jnp.sum(raised, axis=over_dim, keepdims=True)


def shift(at, by, size):
    return lax.rem(at + (by + size), size)


def iota(shape, dim):
    return lax.broadcasted_iota(jnp.int32, shape, dim)


def zero_one(mask):
    return mask.astype(F32).astype(BF16)


def tiled(block, group):
    packed, features = block.shape
    pieces = [
        block[:, at * TILE:(at + 1) * TILE].reshape(group, 1, packed // group, TILE)
        for at in range(features // TILE)
    ]
    if len(pieces) % 2:
        pieces.append(jnp.zeros_like(pieces[0]))
    block = jnp.concatenate(pieces, axis=1)
    return block.reshape(group, len(pieces) * (packed // group), TILE).astype(BF16)


def untiled(block, features):
    group, high, _ = block.shape
    block = block.astype(F32).reshape(group, high // 8, 8, TILE)
    return jnp.concatenate(
        [block[:, at].reshape(group * 8, TILE) for at in range(features // TILE)], axis=1
    ).astype(BF16)


def picker(packed, half, by_member, lead):
    shape = (packed // 2, packed)
    row, column = iota(shape, 0), iota(shape, 1)
    first, source, second = row // (packed // 4), (row % (packed // 4)) // 2, row % 2
    image, member = (second, (first + lead) % 2) if by_member else (first, second)
    return zero_one(column == ((source * 2 + half) * 2 + image) * 2 + member)


def unpack(block, depth, by_member, lead=0):
    block = untiled(block, depth // 2)
    return jnp.concatenate(
        [jnp.dot(picker(block.shape[0], half, by_member, lead), block, preferred_element_type=F32)
         for half in range(2)],
        axis=1,
    ).astype(BF16)


def pack(block, lead):
    rows, depth = block.shape
    return sum(
        lax.dot_general(picker(2 * rows, half, True, lead), block[:, half * depth // 2:(half + 1) * depth // 2],
                        (((0,), (0,)), ((), ())), preferred_element_type=F32)
        for half in range(2)
    )


ORDER = (
    ("enter",), ("ws", 6), ("make", 0), ("ws", 7), ("make", 1), ("ws", 5), ("ws", 4), ("own", 0), ("z1", 0, 0),
    ("b1", 0), ("g1", 0), ("s1", 0, 0), ("ws", 9), ("b2t", 0), ("ws", 0), ("ws", 2), ("own", 1), ("z1", 0, 1),
    ("ws", 8), ("z1", 0, 2), ("z1", 0, 3), ("g2t", 0, 0), ("z2t", 0, 0, 1), ("g2t", 0, 1), ("s1", 0, 1),
    ("z2t", 0, 1, 0), ("s1", 0, 2), ("s2t", 0, 0), ("z2t", 0, 1, 1), ("z2t", 0, 0, 0), ("b1", 1), ("ws", 3),
    ("z2t", 0, 2, 1), ("z2t", 0, 2, 0), ("z2t", 0, 3, 0), ("z2t", 0, 3, 1), ("ws", 1), ("g1", 1), ("s2t", 0, 1),
    ("z1", 1, 0), ("s1", 0, 3), ("b2t", 1), ("zg", 0, 2), ("zg", 0, 3), ("zg", 0, 0), ("g", 0, 0), ("s1", 1, 0),
    ("zg", 0, 1), ("z1", 1, 2), ("s2t", 0, 2), ("z1", 1, 1), ("weights",), ("part", 0, 0), ("s2t", 0, 3),
    ("r1", 0, 0), ("z1", 1, 3), ("g2t", 1, 1), ("s1", 1, 2), ("g", 0, 1), ("g2t", 1, 0), ("part", 0, 1),
    ("s1", 1, 1), ("r1", 0, 1), ("s2t", 1, 0), ("z2t", 1, 0, 1), ("g", 0, 3), ("part", 0, 3), ("r1", 0, 3),
    ("z2t", 1, 0, 0), ("z2t", 1, 2, 1), ("g", 0, 2), ("z2t", 1, 2, 0), ("z2t", 1, 1, 0), ("z2t", 1, 1, 1),
    ("part", 0, 2), ("q1", 0, 2), ("z2t", 1, 3, 1), ("s2t", 1, 2), ("z2t", 1, 3, 0), ("q1", 0, 1), ("q1", 0, 3),
    ("r2t", 0, 3), ("q1", 0, 0), ("s1", 1, 3), ("s2t", 1, 1), ("zg", 1, 0), ("r1", 0, 2), ("q2t", 0, 2, 0),
    ("r2t", 0, 1), ("r2t", 0, 0), ("zg", 1, 2), ("g", 1, 0), ("g", 1, 2), ("q2t", 0, 2, 1), ("zg", 1, 1),
    ("r", 0, 3), ("t1", 0), ("zg", 1, 3), ("part", 1, 0), ("s2t", 1, 3), ("r1", 1, 0), ("q2t", 0, 0, 1),
    ("q2t", 0, 3, 0), ("q2t", 0, 3, 1), ("part", 1, 2), ("r2t", 0, 2), ("q2t", 0, 1, 1), ("r1", 1, 2),
    ("g", 1, 1), ("q2t", 0, 1, 0), ("part", 1, 1), ("r1", 1, 1), ("g", 1, 3), ("q2t", 0, 0, 0), ("part", 1, 3),
    ("q1", 1, 2), ("r", 0, 2), ("q", 0, 2), ("q1", 1, 0), ("q1", 1, 1), ("r", 0, 1), ("q1", 1, 3), ("r1", 1, 3),
    ("r2t", 1, 0), ("weight", 1), ("ds", 1, 4), ("t2t", 0, 1), ("t2t", 0, 0), ("q", 0, 3), ("r2t", 1, 2),
    ("weight", 0), ("r2t", 1, 3), ("v1", 0), ("q2t", 1, 3, 0), ("q", 0, 0), ("ds", 0, 1), ("r", 0, 0),
    ("q2t", 1, 3, 1), ("r", 1, 3), ("r2t", 1, 1), ("ds", 1, 3), ("t1", 1), ("q2t", 1, 2, 1), ("q", 0, 1),
    ("q2t", 1, 2, 0), ("r", 1, 2), ("r", 1, 0), ("q2t", 1, 1, 0), ("q2t", 1, 1, 1), ("v2t", 0),
    ("q2t", 1, 0, 0), ("ds", 0, 4), ("ds", 1, 1), ("q2t", 1, 0, 1), ("q", 1, 3), ("r", 1, 1), ("ds", 0, 2),
    ("v", 0), ("t", 0), ("back", 0), ("q", 1, 2), ("t2t", 1, 1), ("t2t", 1, 0), ("v1", 1), ("ds", 1, 2),
    ("q", 1, 1), ("v2t", 1), ("ds", 0, 0), ("ds", 1, 0), ("q", 1, 0), ("finish", 0), ("ds", 0, 3), ("v", 1),
    ("t", 1), ("back", 1), ("store", 0), ("store", 1), ("finish", 1),
)


def kernel(
    tokens, logits_ref, out_grad, w_in_ref, w_out_ref,
    slot_in_grad_ref, from_combine_ref, w_in_grad_ref, w_out_grad_ref,
    combine, outbox, inbox, back_outbox, back_inbox,
    rows, other, part, other_part, from_twin, last_half, last_full, side_half, side_full, side_twin, total,
    weights, weight_grads, mate_grads, slope, hidden, pre_grad,
    load_sem, store_sem, swap_send, swap_recv, send_sem, recv_sem,
):
    count, depth = rows.shape[3:]
    width = weights.shape[1] // 2
    images, slots, length = combine.shape
    members = 2
    group = slots // members
    packed = group * 2 * images * members
    me = lax.axis_index("dp")
    mine = lax.axis_index("expert")
    z, x = me // RING, lax.rem(me, RING)
    z_to = (shift(z, 1, RING), shift(z, -1, RING))
    z_from = (z_to[1], z_to[0])
    chunk = (z, z_from[0], z_from[1], shift(z, 2, RING))
    z_dev = tuple(to * RING + x for to in z_to)
    turn = lax.rem(mine, 2)
    turned = shift(x, turn, RING)
    mate = shift(turned + 1 - 2 * lax.rem(turned, 2), RING - turn, RING)
    twin = shift(RING - 1 - turned, RING - turn, RING)
    beyond = shift(x, 2, RING)
    places = (x, mate, twin, beyond)
    mate_dev, twin_dev = z * RING + mate, z * RING + twin
    own = lax.rem((turned + 1) // 2, 2)
    first, second = pl.ds(0, SPLIT), pl.ds(SPLIT, depth - SPLIT)
    halves = (pl.ds(0, count // 2), pl.ds(count // 2, count // 2))

    def partner(by):
        return lax.rem(mine + by, group)

    barrier = pltpu.get_barrier_semaphore()
    for there in z_dev + (mate_dev, twin_dev):
        pl.semaphore_signal(barrier, inc=1, device_id={"dp": there}, device_id_type=MESH)

    def greet(by, carry):
        pl.semaphore_signal(barrier, inc=1, device_id={"expert": partner(by)}, device_id_type=MESH)
        return carry

    lax.fori_loop(1, group, greet, 0)

    loads = [
        pltpu.make_async_copy(source.at[own], weights.at[i, pl.ds(0, width)], load_sem.at[i])
        for i, source in enumerate((w_in_ref, w_out_ref))
    ]
    for load in loads:
        load.start()

    def swap_copy(kind, way, by, box, inbound):
        return pltpu.make_async_remote_copy(
            src_ref=box.at[kind, partner(by)], dst_ref=inbound.at[kind, mine],
            send_sem=swap_send.at[way, kind, by], recv_sem=swap_recv.at[way, kind, by],
            device_id={"expert": partner(by)}, device_id_type=MESH,
        )

    def swap_start(kind, way, box, inbound):
        for by in range(1, group):
            swap_copy(kind, way, by, box, inbound).start()
        inbound[kind, mine] = box[kind, mine]

    def swap_arrived(kind, way, box, inbound):
        for by in range(1, group):
            swap_copy(kind, way, by, box, inbound).wait_recv()

    def swap_sent(kind, way, box, inbound):
        for by in range(1, group):
            swap_copy(kind, way, by, box, inbound).wait_send()

    def make_slots(kind):
        source = (tokens, out_grad)[kind]
        left = []
        for image in range(images):
            soft = soft_weights(logits_ref[image], 1 - kind)
            if kind == 1:
                combine[image] = soft
            row, slot = iota((packed, slots), 0), iota((packed, slots), 1)
            spread = zero_one((slot == (row // 8) * 2 + row % 2) & ((row // 2) % 2 == image))
            left.append(jnp.dot(spread, soft.astype(BF16), preferred_element_type=F32).astype(BF16))
        slot = jnp.dot(jnp.concatenate(left, axis=1), source[...].reshape(images * length, depth),
                       preferred_element_type=F32)
        first = (iota((packed, depth // 2), 0) // 4) % 2 == 0
        outbox[kind] = tiled(jnp.where(first, slot[:, :depth // 2], slot[:, depth // 2:]), group)

    def own_rows(kind):
        swap_arrived(kind, 0, outbox, inbox)
        block = unpack(inbox[kind], depth, True, own)
        rows[kind, z, x] = block[:count]
        other[kind, z] = block[count:]

    def send_back(kind):
        back_outbox[kind] = tiled(pack(total[kind].reshape(members * count, depth), own), group)
        swap_start(kind, 1, back_outbox, back_inbox)

    def finish(kind):
        swap_arrived(kind, 1, back_outbox, back_inbox)
        back = unpack(back_inbox[kind], depth, False)
        if kind == 1:
            slot_in_grad_ref[...] = back
            return
        swap_sent(0, 1, back_outbox, back_inbox)
        for image in range(images):
            grad = lax.dot_general(back[image * slots:(image + 1) * slots], out_grad[image],
                                   (((1,), (1,)), ((), ())), preferred_element_type=F32)
            soft = combine[image]
            from_combine_ref[image] = soft * (grad - jnp.sum(soft * grad, axis=0, keepdims=True))

    sent = []
    flying = {}

    def send(key, source, target, there):
        copy = pltpu.make_async_remote_copy(
            src_ref=source, dst_ref=target,
            send_sem=send_sem.at[len(sent)], recv_sem=recv_sem.at[len(sent)],
            device_id={"dp": there}, device_id_type=MESH,
        )
        copy.start()
        sent.append(copy)
        flying[key] = copy

    def arrived(*key):
        flying.pop(key).wait_recv()

    tasks = {}

    def task(*name):
        def keep(run):
            tasks[name] = run
            return run

        return keep

    def gather(kind):
        def z_pieces(at):
            return rows.at[kind, at, x, :, first], other.at[kind, at, :, first]

        @task("g1", kind)
        def _():
            for way in range(2):
                for i, piece in enumerate(z_pieces(z)):
                    send(("g1", kind, way, i), piece, piece, z_dev[way])

        for way in range(2):
            @task("g2t", kind, way)
            def _(way=way):
                for i in range(2):
                    arrived("g1", kind, way, i)
                piece = z_pieces(z_from[way])[way]
                send(("g2", kind, way), piece, piece, z_dev[way])

        def along_x(name, at, features):
            here = rows.at[kind, at, x, :, features]
            send(name + ("twin",), here, here, twin_dev)
            send(name + ("mate",), other.at[kind, at, :, features], here, mate_dev)

        def from_mate(name, at, features):
            arrived(*name, "mate")
            piece = rows.at[kind, at, mate, :, features]
            send(name + ("beyond",), piece, piece, twin_dev)

        for c in range(RING):
            @task("s1", kind, c)
            def _(c=c):
                if c == 3:
                    for way in range(2):
                        arrived("g2", kind, way)
                along_x(("s1", kind, c), chunk[c], first)

            @task("s2t", kind, c)
            def _(c=c):
                from_mate(("s1", kind, c), chunk[c], first)

            @task("g", kind, c)
            def _(c=c):
                arrived("s1", kind, c, "twin")
                arrived("s1", kind, c, "beyond")

        @task("b1", kind)
        def _():
            along_x(("b1", kind), z, second)

        @task("b2t", kind)
        def _():
            from_mate(("b1", kind), z, second)

        for c in range(RING):
            @task("z1", kind, c)
            def _(c=c):
                if c >= 2:
                    arrived("b1", kind, ("twin", "beyond")[c - 2])
                piece = rows.at[kind, z, places[c], :, second]
                for way in range(2):
                    send(("z1", kind, c, way), piece, piece, z_dev[way])

            for way in range(2):
                @task("z2t", kind, c, way)
                def _(c=c, way=way):
                    arrived("z1", kind, c, way)
                    piece = rows.at[kind, z_from[way], places[c], halves[way], second]
                    send(("z2", kind, c, way), piece, piece, z_dev[way])

            @task("zg", kind, c)
            def _(c=c):
                for way in range(2):
                    arrived("z2", kind, c, way)

    def plus(*refs):
        value = refs[0][...].astype(F32)
        for ref in refs[1:]:
            value = value + ref[...].astype(F32)
        return value.astype(BF16)

    def reduce(kind):
        def to_twin(name, at, features, boxes):
            for i, place in enumerate((beyond, twin)):
                send(name + (i,), part.at[kind, at, place, :, features], boxes.at[i], twin_dev)

        def to_mate(name, at, features, boxes):
            arrived(*name, 0)
            piece = part.at[kind, at, mate, :, features]
            piece[...] = plus(piece, boxes.at[0])
            send(name + ("mate",), piece, other_part.at[kind, at, :, features], mate_dev)

        for c in range(RING):
            @task("r1", kind, c)
            def _(c=c):
                to_twin(("r1", kind, c), chunk[c], first, from_twin.at[kind, c])

            @task("r2t", kind, c)
            def _(c=c):
                to_mate(("r1", kind, c), chunk[c], first, from_twin.at[kind, c])

            @task("r", kind, c)
            def _(c=c):
                arrived("r1", kind, c, 1)
                arrived("r1", kind, c, "mate")
                piece = part.at[kind, chunk[c], x, :, first]
                piece[...] = plus(piece, from_twin.at[kind, c, 1])

        def z_pieces(at):
            return part.at[kind, at, x, :, first], other_part.at[kind, at, :, first]

        @task("t1", kind)
        def _():
            for way, piece in enumerate(z_pieces(chunk[3])):
                send(("t1", kind, way), piece, last_half.at[kind, way], z_dev[way])

        for way in range(2):
            @task("t2t", kind, way)
            def _(way=way):
                arrived("t1", kind, way)
                pieces = z_pieces(z_to[way])
                pieces[way][...] = plus(pieces[way], last_half.at[kind, way])
                for i, piece in enumerate(pieces):
                    send(("t2", kind, way, i), piece, last_full.at[kind, way, i], z_dev[way])

        @task("t", kind)
        def _():
            for i, piece in enumerate(z_pieces(z)):
                for way in range(2):
                    arrived("t2", kind, way, i)
                total[kind, i, :, first] = plus(piece, last_full.at[kind, 0, i], last_full.at[kind, 1, i])

        for c in range(RING):
            @task("q1", kind, c)
            def _(c=c):
                for way in range(2):
                    send(("q1", kind, c, way), part.at[kind, chunk[3], places[c], halves[way], second],
                         side_half.at[kind, c, way], z_dev[way])

            for way in range(2):
                @task("q2t", kind, c, way)
                def _(c=c, way=way):
                    arrived("q1", kind, c, way)
                    piece = part.at[kind, z_to[way], places[c], halves[way], second]
                    piece[...] = plus(piece, side_half.at[kind, c, way])
                    send(("q2", kind, c, way), part.at[kind, z_to[way], places[c], :, second],
                         side_full.at[kind, c, way], z_dev[way])

            @task("q", kind, c)
            def _(c=c):
                for way in range(2):
                    arrived("q2", kind, c, way)
                piece = part.at[kind, z, places[c], :, second]
                piece[...] = plus(piece, side_full.at[kind, c, 0], side_full.at[kind, c, 1])

        @task("v1", kind)
        def _():
            to_twin(("v1", kind), z, second, side_twin.at[kind])

        @task("v2t", kind)
        def _():
            to_mate(("v1", kind), z, second, side_twin.at[kind])

        @task("v", kind)
        def _():
            arrived("v1", kind, 1)
            arrived("v1", kind, "mate")
            total[kind, 0, :, second] = plus(part.at[kind, z, x, :, second], side_twin.at[kind, 1])
            total[kind, 1, :, second] = other_part[kind, z, :, second]

    def chunk_rows(kind, c):
        return rows[kind, chunk[c]].reshape(RING * count, depth)

    def place(c):
        return pl.ds(pl.multiple_of(chunk[c] * (RING * count), RING * count), RING * count)

    def forward(c):
        pre = lax.dot_general(chunk_rows(0, c), weights[0], (((1,), (1,)), ((), ())),
                              preferred_element_type=F32)
        cdf = normal_cdf(pre)
        act = (pre * cdf).astype(BF16)
        slope[place(c)] = cdf + pre * jnp.exp(-0.5 * pre * pre) * 0.3989422804014327
        hidden[place(c)] = act
        out = jnp.dot(act, weights[1], preferred_element_type=F32)
        part[0, chunk[c]] = out.astype(BF16).reshape(RING, count, depth)

    def backward(c):
        grad = lax.dot_general(chunk_rows(1, c), weights[1], (((1,), (1,)), ((), ())),
                               preferred_element_type=F32)
        grad = (grad * slope[place(c)]).astype(BF16)
        pre_grad[place(c)] = grad
        out = jnp.dot(grad, weights[0], preferred_element_type=F32)
        part[1, chunk[c]] = out.astype(BF16).reshape(RING, count, depth)

    def weight_grad(kind):
        left = (pre_grad, hidden)[kind][...]
        for part_at in range(2):
            columns = pl.ds(part_at * (depth // 2), depth // 2)
            right = rows[kind, :, :, :, columns].reshape(RING * RING * count, depth // 2)
            weight_grads[kind, :, columns] = lax.dot_general(
                left, right, (((0,), (0,)), ((), ())), preferred_element_type=F32).astype(BF16)

    piece_rows = width // PIECES

    def weight_piece(i):
        matrix, at = i // PIECES, i % PIECES * piece_rows
        send(("w", i), (w_in_ref, w_out_ref)[matrix].at[1 - own, pl.ds(at, piece_rows)],
             weights.at[matrix, pl.ds(width + at, piece_rows)], mate_dev)

    def grad_piece(kind, i):
        at = i * piece_rows
        send(("d", kind, i), weight_grads.at[kind, pl.ds(width + at, piece_rows)],
             mate_grads.at[kind, pl.ds(at, piece_rows)], mate_dev)

    outs = (w_in_grad_ref, w_out_grad_ref)
    stores = []

    def start_store(source, target, sem):
        stores.append(pltpu.make_async_copy(source, target, sem))
        stores[-1].start()

    def store_own(kind):
        start_store(weight_grads.at[kind, pl.ds(0, width)], outs[kind].at[own], store_sem.at[kind, PIECES])

    def store_piece(kind, i):
        arrived("d", kind, i)
        here = pl.ds(i * piece_rows, piece_rows)
        start_store(mate_grads.at[kind, here], outs[kind].at[1 - own, here], store_sem.at[kind, i])

    def store(kind):
        for i in range(PIECES):
            if ("d", kind, i) in flying:
                store_piece(kind, i)

    @task("enter")
    def _():
        make_slots(0)
        pl.semaphore_wait(barrier, 4 + group - 1)

    @task("weights")
    def _():
        for i in range(2 * PIECES):
            arrived("w", i)
        for load in loads:
            load.wait()
        for kind in range(2):
            swap_sent(kind, 0, outbox, inbox)

    for i in range(2 * PIECES):
        tasks["ws", i] = lambda i=i: weight_piece(i)
    for kind in range(2):
        @task("make", kind)
        def _(kind=kind):
            if kind == 1:
                make_slots(1)
            swap_start(kind, 0, outbox, inbox)

        tasks["own", kind] = lambda kind=kind: own_rows(kind)
        gather(kind)
        reduce(kind)
        for c in range(RING):
            tasks["part", kind, c] = lambda kind=kind, c=c: (forward, backward)[kind](c)
        tasks["back", kind] = lambda kind=kind: send_back(kind)
        tasks["finish", kind] = lambda kind=kind: finish(kind)
        @task("weight", kind)
        def _(kind=kind):
            weight_grad(kind)
            store_own(kind)

        for i in range(PIECES):
            tasks["ds", kind, i] = lambda kind=kind, i=i: grad_piece(kind, i)
        tasks["store", kind] = lambda kind=kind: store(kind)

    assert sorted(tasks, key=str) == sorted(ORDER, key=str)
    counts, waited = [], 0
    for at, name in enumerate(ORDER):
        tasks[name]()
        counts.append(len(sent))
        if name in STORE_AT:
            for piece in ORDER[:at + 1 - STORE_AT[name]]:
                if piece[0] == "ds" and ("d",) + piece[1:] in flying:
                    store_piece(*piece[1:])
        while at >= LAG and waited < counts[at - LAG]:
            sent[waited].wait_send()
            waited += 1
    assert not flying and len(sent) == COPIES
    for copy in sent[waited:]:
        copy.wait_send()
    swap_sent(1, 1, back_outbox, back_inbox)
    for copy in stores:
        copy.wait()


def last_kernel(
    tokens, logits_ref, slot_in_grad_ref, from_combine_ref, w_in_grad_ref, w_out_grad_ref,
    token_grad_ref, logit_grad_ref, w_in_out_ref, w_out_out_ref,
    token_grad, sem, token_sem,
):
    images, slots, _ = logits_ref.shape
    moves = [
        pltpu.make_async_copy(source.at[e], target.at[e], sem.at[2 * i + e])
        for i, (source, target) in enumerate(
            ((w_in_grad_ref, w_in_out_ref), (w_out_grad_ref, w_out_out_ref)))
        for e in range(2)
    ]
    for move in moves:
        move.start()
    softs = []
    for image in range(images):
        back = slot_in_grad_ref[image * slots:(image + 1) * slots]
        softs.append(soft_weights(logits_ref[image], 1))
        token_grad[image] = lax.dot_general(
            softs[image].astype(BF16), back, (((0,), (0,)), ((), ())), preferred_element_type=F32
        ).astype(BF16)
        moves.append(pltpu.make_async_copy(token_grad.at[image], token_grad_ref.at[image], token_sem.at[image]))
        moves[-1].start()
    for image in range(images):
        back = slot_in_grad_ref[image * slots:(image + 1) * slots]
        grad = lax.dot_general(back, tokens[image], (((1,), (1,)), ((), ())), preferred_element_type=F32)
        soft = softs[image]
        grad = soft * (grad - jnp.sum(soft * grad, axis=1, keepdims=True))
        logit_grad_ref[image] = from_combine_ref[image] + grad
    for move in moves:
        move.wait()


def shards(tokens, logits, out_grad, w_in, w_out):
    images, length, depth = tokens.shape
    slots = logits.shape[2]
    logits = jnp.transpose(logits, (0, 2, 1))
    members, width, _ = w_in.shape
    group = slots // members
    count = group * images
    kept = (RING * RING * count, 2 * width)
    columns = depth // 2 // TILE
    swapped = (2, group, (columns + columns % 2) * 8, TILE)
    rest = depth - SPLIT
    shape = jax.ShapeDtypeStruct
    whole = pl.BlockSpec(memory_space=pl.ANY)
    inside = pl.BlockSpec(memory_space=pltpu.VMEM)
    far = pl.BlockSpec(memory_space=pltpu.HBM)
    slot_in_grad, from_combine, w_in_grad, w_out_grad = pl.pallas_call(
        kernel,
        out_shape=(
            shape((images * slots, depth), BF16),
            shape(logits.shape, F32),
            shape(w_in.shape, BF16),
            shape(w_out.shape, BF16),
        ),
        in_specs=[inside, inside, inside, far, far],
        out_specs=(inside, inside, whole, whole),
        scratch_shapes=[
            pltpu.VMEM(logits.shape, F32),
            pltpu.VMEM(swapped, BF16),
            pltpu.VMEM(swapped, BF16),
            pltpu.VMEM(swapped, BF16),
            pltpu.VMEM(swapped, BF16),
            pltpu.VMEM((2, RING, RING, count, depth), BF16),
            pltpu.VMEM((2, RING, count, depth), BF16),
            pltpu.VMEM((2, RING, RING, count, depth), BF16),
            pltpu.VMEM((2, RING, count, depth), BF16),
            pltpu.VMEM((2, RING, 2, count, SPLIT), BF16),
            pltpu.VMEM((2, 2, count, SPLIT), BF16),
            pltpu.VMEM((2, 2, 2, count, SPLIT), BF16),
            pltpu.VMEM((2, RING, 2, count // 2, rest), BF16),
            pltpu.VMEM((2, RING, 2, count, rest), BF16),
            pltpu.VMEM((2, 2, count, rest), BF16),
            pltpu.VMEM((2, 2, count, depth), BF16),
            pltpu.VMEM((2, 2 * width, depth), BF16),
            pltpu.VMEM((2, 2 * width, depth), BF16),
            pltpu.VMEM((2, width, depth), BF16),
            pltpu.VMEM(kept, F32),
            pltpu.VMEM(kept, BF16),
            pltpu.VMEM(kept, BF16),
            pltpu.SemaphoreType.DMA((2,)),
            pltpu.SemaphoreType.DMA((2, PIECES + 1)),
            pltpu.SemaphoreType.DMA((2, 2, group)),
            pltpu.SemaphoreType.DMA((2, 2, group)),
            pltpu.SemaphoreType.DMA((COPIES,)),
            pltpu.SemaphoreType.DMA((COPIES,)),
        ],
        compiler_params=pltpu.CompilerParams(
            collective_id=0, has_side_effects=True, vmem_limit_bytes=48 * 2**20
        ),
    )(tokens, logits, out_grad, w_in, w_out)
    token_grad, logit_grad, w_in_grad, w_out_grad = pl.pallas_call(
        last_kernel,
        out_shape=(
            shape(tokens.shape, BF16),
            shape(logits.shape, F32),
            shape(w_in.shape, BF16),
            shape(w_out.shape, BF16),
        ),
        in_specs=[inside, inside, inside, inside, whole, whole],
        out_specs=(whole, inside, whole, whole),
        scratch_shapes=[
            pltpu.VMEM(tokens.shape, BF16),
            pltpu.SemaphoreType.DMA((4,)),
            pltpu.SemaphoreType.DMA((2,)),
        ],
        compiler_params=pltpu.CompilerParams(vmem_limit_bytes=16 * 2**20),
    )(tokens, logits, slot_in_grad, from_combine, w_in_grad, w_out_grad)
    return token_grad, jnp.transpose(logit_grad, (0, 2, 1)), w_in_grad, w_out_grad


def solution(mesh):
    placed = (
        P(("dp", "expert"), None, None),
        P(("dp", "expert"), None, None),
        P(("dp", "expert"), None, None),
        P("expert", "dp", None),
        P("expert", "dp", None),
    )
    return jax.shard_map(
        shards,
        mesh=mesh,
        in_specs=placed,
        out_specs=(
            P(("dp", "expert"), None, None),
            P(("dp", "expert"), None, None),
            P("expert", "dp", None),
            P("expert", "dp", None),
        ),
        check_vma=False,
    )
```

```python
import jax
import jax.numpy as jnp
from jax import lax
from jax.experimental import pallas as pl
from jax.experimental.pallas import tpu as pltpu
from jax.sharding import PartitionSpec as P

RING = 4
TILE = 128
SPLIT = 768
LAG = 90
PIECES = 5
COPIES = 2 * 74 + 4 * PIECES
MESH = pl.DeviceIdType.MESH
BF16 = jnp.bfloat16
F32 = jnp.float32


def normal_cdf(values):
    return 0.5 * (1.0 + lax.erf(values * 0.7071067811865476))


def soft_weights(values, over_dim):
    highest = jnp.max(values, axis=over_dim, keepdims=True)
    raised = jnp.exp(values - highest)
    return raised / jnp.sum(raised, axis=over_dim, keepdims=True)


def shift(at, by, size):
    return lax.rem(at + (by + size), size)


def iota(shape, dim):
    return lax.broadcasted_iota(jnp.int32, shape, dim)


def zero_one(mask):
    return mask.astype(F32).astype(BF16)


def tiled(block, group):
    packed, features = block.shape
    pieces = [
        block[:, at * TILE:(at + 1) * TILE].reshape(group, 1, packed // group, TILE)
        for at in range(features // TILE)
    ]
    if len(pieces) % 2:
        pieces.append(jnp.zeros_like(pieces[0]))
    block = jnp.concatenate(pieces, axis=1)
    return block.reshape(group, len(pieces) * (packed // group), TILE).astype(BF16)


def untiled(block, features):
    group, high, _ = block.shape
    block = block.astype(F32).reshape(group, high // 8, 8, TILE)
    return jnp.concatenate(
        [block[:, at].reshape(group * 8, TILE) for at in range(features // TILE)], axis=1
    ).astype(BF16)


def picker(packed, half, by_member, lead):
    shape = (packed // 2, packed)
    row, column = iota(shape, 0), iota(shape, 1)
    first, source, second = row // (packed // 4), (row % (packed // 4)) // 2, row % 2
    image, member = (second, (first + lead) % 2) if by_member else (first, second)
    return zero_one(column == ((source * 2 + half) * 2 + image) * 2 + member)


def unpack(block, depth, by_member, lead=0):
    block = untiled(block, depth // 2)
    return jnp.concatenate(
        [jnp.dot(picker(block.shape[0], half, by_member, lead), block, preferred_element_type=F32)
         for half in range(2)],
        axis=1,
    ).astype(BF16)


def pack(block, lead):
    rows, depth = block.shape
    return sum(
        lax.dot_general(picker(2 * rows, half, True, lead), block[:, half * depth // 2:(half + 1) * depth // 2],
                        (((0,), (0,)), ((), ())), preferred_element_type=F32)
        for half in range(2)
    )


ORDER = (
    ("enter",), ("ws", 6), ("make", 0), ("ws", 7), ("make", 1), ("ws", 5), ("ws", 4), ("own", 0), ("z1", 0, 0),
    ("b1", 0), ("g1", 0), ("s1", 0, 0), ("ws", 9), ("b2t", 0), ("ws", 0), ("ws", 2), ("own", 1), ("z1", 0, 1),
    ("ws", 8), ("z1", 0, 2), ("z1", 0, 3), ("g2t", 0, 0), ("z2t", 0, 0, 1), ("g2t", 0, 1), ("s1", 0, 1),
    ("z2t", 0, 1, 0), ("s1", 0, 2), ("s2t", 0, 0), ("z2t", 0, 1, 1), ("z2t", 0, 0, 0), ("b1", 1), ("ws", 3),
    ("z2t", 0, 2, 1), ("z2t", 0, 2, 0), ("z2t", 0, 3, 0), ("z2t", 0, 3, 1), ("ws", 1), ("g1", 1), ("s2t", 0, 1),
    ("z1", 1, 0), ("s1", 0, 3), ("b2t", 1), ("zg", 0, 2), ("zg", 0, 3), ("zg", 0, 0), ("g", 0, 0), ("s1", 1, 0),
    ("zg", 0, 1), ("z1", 1, 2), ("s2t", 0, 2), ("z1", 1, 1), ("weights",), ("part", 0, 0), ("s2t", 0, 3),
    ("r1", 0, 0), ("z1", 1, 3), ("g2t", 1, 1), ("s1", 1, 2), ("g", 0, 1), ("g2t", 1, 0), ("part", 0, 1),
    ("s1", 1, 1), ("r1", 0, 1), ("s2t", 1, 0), ("z2t", 1, 0, 1), ("g", 0, 3), ("part", 0, 3), ("r1", 0, 3),
    ("z2t", 1, 0, 0), ("z2t", 1, 2, 1), ("g", 0, 2), ("z2t", 1, 2, 0), ("z2t", 1, 1, 0), ("z2t", 1, 1, 1),
    ("part", 0, 2), ("q1", 0, 2), ("z2t", 1, 3, 1), ("s2t", 1, 2), ("z2t", 1, 3, 0), ("q1", 0, 1), ("q1", 0, 3),
    ("r2t", 0, 3), ("q1", 0, 0), ("s1", 1, 3), ("s2t", 1, 1), ("zg", 1, 0), ("r1", 0, 2), ("q2t", 0, 2, 0),
    ("r2t", 0, 1), ("r2t", 0, 0), ("zg", 1, 2), ("g", 1, 0), ("g", 1, 2), ("q2t", 0, 2, 1), ("zg", 1, 1),
    ("r", 0, 3), ("t1", 0), ("zg", 1, 3), ("part", 1, 0), ("s2t", 1, 3), ("r1", 1, 0), ("q2t", 0, 0, 1),
    ("q2t", 0, 3, 0), ("q2t", 0, 3, 1), ("part", 1, 2), ("r2t", 0, 2), ("q2t", 0, 1, 1), ("r1", 1, 2),
    ("g", 1, 1), ("q2t", 0, 1, 0), ("part", 1, 1), ("r1", 1, 1), ("g", 1, 3), ("q2t", 0, 0, 0), ("part", 1, 3),
    ("q1", 1, 2), ("r", 0, 2), ("q", 0, 2), ("q1", 1, 0), ("q1", 1, 1), ("r", 0, 1), ("q1", 1, 3), ("r1", 1, 3),
    ("r2t", 1, 0), ("weight", 1), ("ds", 1, 4), ("t2t", 0, 1), ("t2t", 0, 0), ("q", 0, 3), ("r2t", 1, 2),
    ("weight", 0), ("r2t", 1, 3), ("v1", 0), ("q2t", 1, 3, 0), ("q", 0, 0), ("ds", 0, 1), ("r", 0, 0),
    ("q2t", 1, 3, 1), ("r", 1, 3), ("r2t", 1, 1), ("ds", 1, 3), ("t1", 1), ("q2t", 1, 2, 1), ("q", 0, 1),
    ("q2t", 1, 2, 0), ("r", 1, 2), ("r", 1, 0), ("q2t", 1, 1, 0), ("q2t", 1, 1, 1), ("v2t", 0),
    ("q2t", 1, 0, 0), ("ds", 0, 4), ("ds", 1, 1), ("q2t", 1, 0, 1), ("q", 1, 3), ("r", 1, 1), ("ds", 0, 2),
    ("v", 0), ("t", 0), ("back", 0), ("q", 1, 2), ("t2t", 1, 1), ("t2t", 1, 0), ("v1", 1), ("ds", 1, 2),
    ("q", 1, 1), ("v2t", 1), ("ds", 0, 0), ("ds", 1, 0), ("q", 1, 0), ("finish", 0), ("ds", 0, 3), ("v", 1),
    ("t", 1), ("back", 1), ("store", 0), ("store", 1), ("finish", 1),
)


def kernel(
    tokens, logits_ref, out_grad, w_in_ref, w_out_ref,
    slot_in_grad_ref, from_combine_ref, w_in_grad_ref, w_out_grad_ref,
    combine, outbox, inbox, back_outbox, back_inbox,
    rows, other, part, other_part, from_twin, last_half, last_full, side_half, side_full, side_twin, total,
    weights, weight_grads, mate_grads, slope, hidden, pre_grad,
    load_sem, store_sem, swap_send, swap_recv, send_sem, recv_sem,
):
    count, depth = rows.shape[3:]
    width = weights.shape[1] // 2
    images, slots, length = combine.shape
    members = 2
    group = slots // members
    packed = group * 2 * images * members
    me = lax.axis_index("dp")
    mine = lax.axis_index("expert")
    z, x = me // RING, lax.rem(me, RING)
    z_to = (shift(z, 1, RING), shift(z, -1, RING))
    z_from = (z_to[1], z_to[0])
    chunk = (z, z_from[0], z_from[1], shift(z, 2, RING))
    z_dev = tuple(to * RING + x for to in z_to)
    turn = lax.rem(mine, 2)
    turned = shift(x, turn, RING)
    mate = shift(turned + 1 - 2 * lax.rem(turned, 2), RING - turn, RING)
    twin = shift(RING - 1 - turned, RING - turn, RING)
    beyond = shift(x, 2, RING)
    places = (x, mate, twin, beyond)
    mate_dev, twin_dev = z * RING + mate, z * RING + twin
    own = lax.rem((turned + 1) // 2, 2)
    first, second = pl.ds(0, SPLIT), pl.ds(SPLIT, depth - SPLIT)
    halves = (pl.ds(0, count // 2), pl.ds(count // 2, count // 2))

    def partner(by):
        return lax.rem(mine + by, group)

    barrier = pltpu.get_barrier_semaphore()
    for there in z_dev + (mate_dev, twin_dev):
        pl.semaphore_signal(barrier, inc=1, device_id={"dp": there}, device_id_type=MESH)

    def greet(by, carry):
        pl.semaphore_signal(barrier, inc=1, device_id={"expert": partner(by)}, device_id_type=MESH)
        return carry

    lax.fori_loop(1, group, greet, 0)

    loads = [
        pltpu.make_async_copy(source.at[own], weights.at[i, pl.ds(0, width)], load_sem.at[i])
        for i, source in enumerate((w_in_ref, w_out_ref))
    ]
    for load in loads:
        load.start()

    def swap_copy(kind, way, by, box, inbound):
        return pltpu.make_async_remote_copy(
            src_ref=box.at[kind, partner(by)], dst_ref=inbound.at[kind, mine],
            send_sem=swap_send.at[way, kind, by], recv_sem=swap_recv.at[way, kind, by],
            device_id={"expert": partner(by)}, device_id_type=MESH,
        )

    def swap_start(kind, way, box, inbound):
        for by in sorted(range(1, group), key=lambda by: -min(by // 2 % RING, RING - by // 2 % RING)):
            swap_copy(kind, way, by, box, inbound).start()
        inbound[kind, mine] = box[kind, mine]

    def swap_arrived(kind, way, box, inbound):
        for by in range(1, group):
            swap_copy(kind, way, by, box, inbound).wait_recv()

    def swap_sent(kind, way, box, inbound):
        for by in range(1, group):
            swap_copy(kind, way, by, box, inbound).wait_send()

    def make_slots(kind):
        source = (tokens, out_grad)[kind]
        left = []
        for image in range(images):
            soft = soft_weights(logits_ref[image], 1 - kind)
            if kind == 1:
                combine[image] = soft
            row, slot = iota((packed, slots), 0), iota((packed, slots), 1)
            spread = zero_one((slot == (row // 8) * 2 + row % 2) & ((row // 2) % 2 == image))
            left.append(jnp.dot(spread, soft.astype(BF16), preferred_element_type=F32).astype(BF16))
        slot = jnp.dot(jnp.concatenate(left, axis=1), source[...].reshape(images * length, depth),
                       preferred_element_type=F32)
        first = (iota((packed, depth // 2), 0) // 4) % 2 == 0
        outbox[kind] = tiled(jnp.where(first, slot[:, :depth // 2], slot[:, depth // 2:]), group)

    def own_rows(kind):
        swap_arrived(kind, 0, outbox, inbox)
        block = unpack(inbox[kind], depth, True, own)
        rows[kind, z, x] = block[:count]
        other[kind, z] = block[count:]

    def send_back(kind):
        back_outbox[kind] = tiled(pack(total[kind].reshape(members * count, depth), own), group)
        swap_start(kind, 1, back_outbox, back_inbox)

    def finish(kind):
        swap_arrived(kind, 1, back_outbox, back_inbox)
        back = unpack(back_inbox[kind], depth, False)
        if kind == 1:
            slot_in_grad_ref[...] = back
            return
        swap_sent(0, 1, back_outbox, back_inbox)
        for image in range(images):
            grad = lax.dot_general(back[image * slots:(image + 1) * slots], out_grad[image],
                                   (((1,), (1,)), ((), ())), preferred_element_type=F32)
            soft = combine[image]
            from_combine_ref[image] = soft * (grad - jnp.sum(soft * grad, axis=0, keepdims=True))

    sent = []
    flying = {}

    def send(key, source, target, there):
        copy = pltpu.make_async_remote_copy(
            src_ref=source, dst_ref=target,
            send_sem=send_sem.at[len(sent)], recv_sem=recv_sem.at[len(sent)],
            device_id={"dp": there}, device_id_type=MESH,
        )
        copy.start()
        sent.append(copy)
        flying[key] = copy

    def arrived(*key):
        flying.pop(key).wait_recv()

    tasks = {}

    def task(*name):
        def keep(run):
            tasks[name] = run
            return run

        return keep

    def gather(kind):
        def z_pieces(at):
            return rows.at[kind, at, x, :, first], other.at[kind, at, :, first]

        @task("g1", kind)
        def _():
            for way in range(2):
                for i, piece in enumerate(z_pieces(z)):
                    send(("g1", kind, way, i), piece, piece, z_dev[way])

        for way in range(2):
            @task("g2t", kind, way)
            def _(way=way):
                for i in range(2):
                    arrived("g1", kind, way, i)
                piece = z_pieces(z_from[way])[way]
                send(("g2", kind, way), piece, piece, z_dev[way])

        def along_x(name, at, features):
            here = rows.at[kind, at, x, :, features]
            send(name + ("twin",), here, here, twin_dev)
            send(name + ("mate",), other.at[kind, at, :, features], here, mate_dev)

        def from_mate(name, at, features):
            arrived(*name, "mate")
            piece = rows.at[kind, at, mate, :, features]
            send(name + ("beyond",), piece, piece, twin_dev)

        for c in range(RING):
            @task("s1", kind, c)
            def _(c=c):
                if c == 3:
                    for way in range(2):
                        arrived("g2", kind, way)
                along_x(("s1", kind, c), chunk[c], first)

            @task("s2t", kind, c)
            def _(c=c):
                from_mate(("s1", kind, c), chunk[c], first)

            @task("g", kind, c)
            def _(c=c):
                arrived("s1", kind, c, "twin")
                arrived("s1", kind, c, "beyond")

        @task("b1", kind)
        def _():
            along_x(("b1", kind), z, second)

        @task("b2t", kind)
        def _():
            from_mate(("b1", kind), z, second)

        for c in range(RING):
            @task("z1", kind, c)
            def _(c=c):
                if c >= 2:
                    arrived("b1", kind, ("twin", "beyond")[c - 2])
                piece = rows.at[kind, z, places[c], :, second]
                for way in range(2):
                    send(("z1", kind, c, way), piece, piece, z_dev[way])

            for way in range(2):
                @task("z2t", kind, c, way)
                def _(c=c, way=way):
                    arrived("z1", kind, c, way)
                    piece = rows.at[kind, z_from[way], places[c], halves[way], second]
                    send(("z2", kind, c, way), piece, piece, z_dev[way])

            @task("zg", kind, c)
            def _(c=c):
                for way in range(2):
                    arrived("z2", kind, c, way)

    def plus(*refs):
        value = refs[0][...].astype(F32)
        for ref in refs[1:]:
            value = value + ref[...].astype(F32)
        return value.astype(BF16)

    def reduce(kind):
        def to_twin(name, at, features, boxes):
            for i, place in enumerate((beyond, twin)):
                send(name + (i,), part.at[kind, at, place, :, features], boxes.at[i], twin_dev)

        def to_mate(name, at, features, boxes):
            arrived(*name, 0)
            piece = part.at[kind, at, mate, :, features]
            piece[...] = plus(piece, boxes.at[0])
            send(name + ("mate",), piece, other_part.at[kind, at, :, features], mate_dev)

        for c in range(RING):
            @task("r1", kind, c)
            def _(c=c):
                to_twin(("r1", kind, c), chunk[c], first, from_twin.at[kind, c])

            @task("r2t", kind, c)
            def _(c=c):
                to_mate(("r1", kind, c), chunk[c], first, from_twin.at[kind, c])

            @task("r", kind, c)
            def _(c=c):
                arrived("r1", kind, c, 1)
                arrived("r1", kind, c, "mate")
                piece = part.at[kind, chunk[c], x, :, first]
                piece[...] = plus(piece, from_twin.at[kind, c, 1])

        def z_pieces(at):
            return part.at[kind, at, x, :, first], other_part.at[kind, at, :, first]

        @task("t1", kind)
        def _():
            for way, piece in enumerate(z_pieces(chunk[3])):
                send(("t1", kind, way), piece, last_half.at[kind, way], z_dev[way])

        for way in range(2):
            @task("t2t", kind, way)
            def _(way=way):
                arrived("t1", kind, way)
                pieces = z_pieces(z_to[way])
                pieces[way][...] = plus(pieces[way], last_half.at[kind, way])
                for i, piece in enumerate(pieces):
                    send(("t2", kind, way, i), piece, last_full.at[kind, way, i], z_dev[way])

        @task("t", kind)
        def _():
            for i, piece in enumerate(z_pieces(z)):
                for way in range(2):
                    arrived("t2", kind, way, i)
                total[kind, i, :, first] = plus(piece, last_full.at[kind, 0, i], last_full.at[kind, 1, i])

        for c in range(RING):
            @task("q1", kind, c)
            def _(c=c):
                for way in range(2):
                    send(("q1", kind, c, way), part.at[kind, chunk[3], places[c], halves[way], second],
                         side_half.at[kind, c, way], z_dev[way])

            for way in range(2):
                @task("q2t", kind, c, way)
                def _(c=c, way=way):
                    arrived("q1", kind, c, way)
                    piece = part.at[kind, z_to[way], places[c], halves[way], second]
                    piece[...] = plus(piece, side_half.at[kind, c, way])
                    send(("q2", kind, c, way), part.at[kind, z_to[way], places[c], :, second],
                         side_full.at[kind, c, way], z_dev[way])

            @task("q", kind, c)
            def _(c=c):
                for way in range(2):
                    arrived("q2", kind, c, way)
                piece = part.at[kind, z, places[c], :, second]
                piece[...] = plus(piece, side_full.at[kind, c, 0], side_full.at[kind, c, 1])

        @task("v1", kind)
        def _():
            to_twin(("v1", kind), z, second, side_twin.at[kind])

        @task("v2t", kind)
        def _():
            to_mate(("v1", kind), z, second, side_twin.at[kind])

        @task("v", kind)
        def _():
            arrived("v1", kind, 1)
            arrived("v1", kind, "mate")
            total[kind, 0, :, second] = plus(part.at[kind, z, x, :, second], side_twin.at[kind, 1])
            total[kind, 1, :, second] = other_part[kind, z, :, second]

    def chunk_rows(kind, c):
        return rows[kind, chunk[c]].reshape(RING * count, depth)

    def place(c):
        return pl.ds(pl.multiple_of(chunk[c] * (RING * count), RING * count), RING * count)

    def forward(c):
        pre = lax.dot_general(chunk_rows(0, c), weights[0], (((1,), (1,)), ((), ())),
                              preferred_element_type=F32)
        cdf = normal_cdf(pre)
        act = (pre * cdf).astype(BF16)
        slope[place(c)] = cdf + pre * jnp.exp(-0.5 * pre * pre) * 0.3989422804014327
        hidden[place(c)] = act
        out = jnp.dot(act, weights[1], preferred_element_type=F32)
        part[0, chunk[c]] = out.astype(BF16).reshape(RING, count, depth)

    def backward(c):
        grad = lax.dot_general(chunk_rows(1, c), weights[1], (((1,), (1,)), ((), ())),
                               preferred_element_type=F32)
        grad = (grad * slope[place(c)]).astype(BF16)
        pre_grad[place(c)] = grad
        out = jnp.dot(grad, weights[0], preferred_element_type=F32)
        part[1, chunk[c]] = out.astype(BF16).reshape(RING, count, depth)

    def weight_grad(kind):
        left = (pre_grad, hidden)[kind][...]
        for part_at in range(2):
            columns = pl.ds(part_at * (depth // 2), depth // 2)
            right = rows[kind, :, :, :, columns].reshape(RING * RING * count, depth // 2)
            weight_grads[kind, :, columns] = lax.dot_general(
                left, right, (((0,), (0,)), ((), ())), preferred_element_type=F32).astype(BF16)

    piece_rows = width // PIECES

    def weight_piece(i):
        matrix, at = i // PIECES, i % PIECES * piece_rows
        send(("w", i), (w_in_ref, w_out_ref)[matrix].at[1 - own, pl.ds(at, piece_rows)],
             weights.at[matrix, pl.ds(width + at, piece_rows)], mate_dev)

    def grad_piece(kind, i):
        at = i * piece_rows
        send(("d", kind, i), weight_grads.at[kind, pl.ds(width + at, piece_rows)],
             mate_grads.at[kind, pl.ds(at, piece_rows)], mate_dev)

    outs = (w_in_grad_ref, w_out_grad_ref)
    stores = []

    def store(kind):
        for i in range(PIECES):
            arrived("d", kind, i)
        for i, source in enumerate((weight_grads.at[kind, pl.ds(0, width)], mate_grads.at[kind])):
            stores.append(pltpu.make_async_copy(
                source, outs[kind].at[(own, 1 - own)[i]], store_sem.at[kind, i]))
            stores[-1].start()

    @task("enter")
    def _():
        make_slots(0)
        pl.semaphore_wait(barrier, 4 + group - 1)

    @task("weights")
    def _():
        for i in range(2 * PIECES):
            arrived("w", i)
        for load in loads:
            load.wait()
        for kind in range(2):
            swap_sent(kind, 0, outbox, inbox)

    for i in range(2 * PIECES):
        tasks["ws", i] = lambda i=i: weight_piece(i)
    for kind in range(2):
        @task("make", kind)
        def _(kind=kind):
            if kind == 1:
                make_slots(1)
            swap_start(kind, 0, outbox, inbox)

        tasks["own", kind] = lambda kind=kind: own_rows(kind)
        gather(kind)
        reduce(kind)
        for c in range(RING):
            tasks["part", kind, c] = lambda kind=kind, c=c: (forward, backward)[kind](c)
        tasks["back", kind] = lambda kind=kind: send_back(kind)
        tasks["finish", kind] = lambda kind=kind: finish(kind)
        tasks["weight", kind] = lambda kind=kind: weight_grad(kind)
        for i in range(PIECES):
            tasks["ds", kind, i] = lambda kind=kind, i=i: grad_piece(kind, i)
        tasks["store", kind] = lambda kind=kind: store(kind)

    assert sorted(tasks, key=str) == sorted(ORDER, key=str)
    counts, waited = [], 0
    for at, name in enumerate(ORDER):
        tasks[name]()
        counts.append(len(sent))
        while at >= LAG and waited < counts[at - LAG]:
            sent[waited].wait_send()
            waited += 1
    assert not flying and len(sent) == COPIES
    for copy in sent[waited:]:
        copy.wait_send()
    swap_sent(1, 1, back_outbox, back_inbox)
    for copy in stores:
        copy.wait()


def last_kernel(
    tokens, logits_ref, slot_in_grad_ref, from_combine_ref, w_in_grad_ref, w_out_grad_ref,
    token_grad_ref, logit_grad_ref, w_in_out_ref, w_out_out_ref,
    token_grad, sem, token_sem,
):
    images, slots, _ = logits_ref.shape
    moves = [
        pltpu.make_async_copy(source.at[e], target.at[e], sem.at[2 * i + e])
        for i, (source, target) in enumerate(
            ((w_in_grad_ref, w_in_out_ref), (w_out_grad_ref, w_out_out_ref)))
        for e in range(2)
    ]
    for move in moves:
        move.start()
    softs = []
    for image in range(images):
        back = slot_in_grad_ref[image * slots:(image + 1) * slots]
        softs.append(soft_weights(logits_ref[image], 1))
        token_grad[image] = lax.dot_general(
            softs[image].astype(BF16), back, (((0,), (0,)), ((), ())), preferred_element_type=F32
        ).astype(BF16)
        moves.append(pltpu.make_async_copy(token_grad.at[image], token_grad_ref.at[image], token_sem.at[image]))
        moves[-1].start()
    for image in range(images):
        back = slot_in_grad_ref[image * slots:(image + 1) * slots]
        grad = lax.dot_general(back, tokens[image], (((1,), (1,)), ((), ())), preferred_element_type=F32)
        soft = softs[image]
        grad = soft * (grad - jnp.sum(soft * grad, axis=1, keepdims=True))
        logit_grad_ref[image] = from_combine_ref[image] + grad
    for move in moves:
        move.wait()


def shards(tokens, logits, out_grad, w_in, w_out):
    images, length, depth = tokens.shape
    slots = logits.shape[2]
    logits = jnp.transpose(logits, (0, 2, 1))
    members, width, _ = w_in.shape
    group = slots // members
    count = group * images
    kept = (RING * RING * count, 2 * width)
    columns = depth // 2 // TILE
    swapped = (2, group, (columns + columns % 2) * 8, TILE)
    rest = depth - SPLIT
    shape = jax.ShapeDtypeStruct
    whole = pl.BlockSpec(memory_space=pl.ANY)
    inside = pl.BlockSpec(memory_space=pltpu.VMEM)
    far = pl.BlockSpec(memory_space=pltpu.HBM)
    slot_in_grad, from_combine, w_in_grad, w_out_grad = pl.pallas_call(
        kernel,
        out_shape=(
            shape((images * slots, depth), BF16),
            shape(logits.shape, F32),
            shape(w_in.shape, BF16),
            shape(w_out.shape, BF16),
        ),
        in_specs=[inside, inside, inside, far, far],
        out_specs=(inside, inside, whole, whole),
        scratch_shapes=[
            pltpu.VMEM(logits.shape, F32),
            pltpu.VMEM(swapped, BF16),
            pltpu.VMEM(swapped, BF16),
            pltpu.VMEM(swapped, BF16),
            pltpu.VMEM(swapped, BF16),
            pltpu.VMEM((2, RING, RING, count, depth), BF16),
            pltpu.VMEM((2, RING, count, depth), BF16),
            pltpu.VMEM((2, RING, RING, count, depth), BF16),
            pltpu.VMEM((2, RING, count, depth), BF16),
            pltpu.VMEM((2, RING, 2, count, SPLIT), BF16),
            pltpu.VMEM((2, 2, count, SPLIT), BF16),
            pltpu.VMEM((2, 2, 2, count, SPLIT), BF16),
            pltpu.VMEM((2, RING, 2, count // 2, rest), BF16),
            pltpu.VMEM((2, RING, 2, count, rest), BF16),
            pltpu.VMEM((2, 2, count, rest), BF16),
            pltpu.VMEM((2, 2, count, depth), BF16),
            pltpu.VMEM((2, 2 * width, depth), BF16),
            pltpu.VMEM((2, 2 * width, depth), BF16),
            pltpu.VMEM((2, width, depth), BF16),
            pltpu.VMEM(kept, F32),
            pltpu.VMEM(kept, BF16),
            pltpu.VMEM(kept, BF16),
            pltpu.SemaphoreType.DMA((2,)),
            pltpu.SemaphoreType.DMA((2, 2)),
            pltpu.SemaphoreType.DMA((2, 2, group)),
            pltpu.SemaphoreType.DMA((2, 2, group)),
            pltpu.SemaphoreType.DMA((COPIES,)),
            pltpu.SemaphoreType.DMA((COPIES,)),
        ],
        compiler_params=pltpu.CompilerParams(
            collective_id=0, has_side_effects=True, vmem_limit_bytes=48 * 2**20
        ),
    )(tokens, logits, out_grad, w_in, w_out)
    token_grad, logit_grad, w_in_grad, w_out_grad = pl.pallas_call(
        last_kernel,
        out_shape=(
            shape(tokens.shape, BF16),
            shape(logits.shape, F32),
            shape(w_in.shape, BF16),
            shape(w_out.shape, BF16),
        ),
        in_specs=[inside, inside, inside, inside, whole, whole],
        out_specs=(whole, inside, whole, whole),
        scratch_shapes=[
            pltpu.VMEM(tokens.shape, BF16),
            pltpu.SemaphoreType.DMA((4,)),
            pltpu.SemaphoreType.DMA((2,)),
        ],
        compiler_params=pltpu.CompilerParams(vmem_limit_bytes=16 * 2**20),
    )(tokens, logits, slot_in_grad, from_combine, w_in_grad, w_out_grad)
    return token_grad, jnp.transpose(logit_grad, (0, 2, 1)), w_in_grad, w_out_grad


def solution(mesh):
    placed = (
        P(("dp", "expert"), None, None),
        P(("dp", "expert"), None, None),
        P(("dp", "expert"), None, None),
        P("expert", "dp", None),
        P("expert", "dp", None),
    )
    return jax.shard_map(
        shards,
        mesh=mesh,
        in_specs=placed,
        out_specs=(
            P(("dp", "expert"), None, None),
            P(("dp", "expert"), None, None),
            P("expert", "dp", None),
            P("expert", "dp", None),
        ),
        check_vma=False,
    )
```
